256 devices in a mesh: dp: 8 (over x, core), expert: 32 (over y, z).
Axes of the slice: x: 4, y: 4, z: 8, core: 2. Of those that a mesh axis runs over, the one named last changes fastest.
Arguments:
- tokens: bfloat16 [32768, 2048], P(('dp', 'expert')), may hold values from -6 to 6
- cotangent: bfloat16 [32768, 2048], P(('dp', 'expert')), may hold values from -1.5 to 1.5
- routing: int32 [32768, 2], P(('dp', 'expert')), may hold values from 0 to 19, all different within a row; in each aligned block of 128 rows (0 to 127, 128 to 255, ...) at most 16 rows name the same one
- gates: bfloat16 [32768, 2], P(('dp', 'expert')), may hold values from 0.19921875 to 1
- new_place: int32 [32], replicated, may hold values from 0 to 19, as said below
- old_place: int32 [20], replicated, may hold values from 0 to 19, each once
- weights: bfloat16 [3, 20, 2048, 768], P(None, None, ('dp', 'expert')), may hold values from -0.125 to 0.125
- first_moment: float32 [3, 20, 2048, 768], P(None, None, ('dp', 'expert')), may hold values from -6 to 6
- second_moment: float32 [3, 20, 2048, 768], P(None, None, ('dp', 'expert')), may hold values from 0.5 to 20
Outputs:
- input_grad: bfloat16 [32768, 2048], P(('dp', 'expert'))
- gate_grad: bfloat16 [32768, 2], P(('dp', 'expert'))
- slot_weights: bfloat16 [3, 32, 2048, 768], P(None, 'expert', 'dp')
- new_first: float32 [3, 20, 2048, 768], P(None, None, ('dp', 'expert'))
- new_second: float32 [3, 20, 2048, 768], P(None, None, ('dp', 'expert'))
The draws below stay inside these ranges and needn't reach their ends.
Inputs may be any that keep to these rules, and one draw needn't show every extreme that they name: `routing`: A token's 2 experts differ; among the 128 tokens of one device no expert is named more than 16 times, a bound that some block reaches. `new_place`: every expert is served by one slot or more. `old_place`: each expert names exactly one row.
All inputs are finite; a program needn't handle non-finite values.
Results may differ from the reference program's by a relative error of at most 0.024.
Values may be sent and summed in bfloat16 or wider, within the bound.
No kernel may reach another device: no remote copies, remote signals or barrier semaphores. Data moves between devices by JAX's collectives and lax.ppermute only.
A program may use at most 128 MiB of HBM per device.

```python
import math
import jax
import jax.numpy as jnp
import numpy as np
from jax import lax

D = 2048
H = 768
TOPK = 2
TOK_DEV = 128
EXPERTS = 20
MOST = 16
TOKENS = 32768
N_DP = 8
N_EXPERT = 32


def draw_new_place(key, part):
    key = jax.random.fold_in(key, 11)
    key_first, key_second, key_third = jax.random.split(key, 3)
    covering = jax.random.permutation(key_first, EXPERTS).astype(jnp.int32)
    extra = jax.random.randint(key_second, (N_EXPERT - EXPERTS,), 0, EXPERTS).astype(jnp.int32)
    joined = jnp.concatenate([covering, extra], axis=0)
    return jax.random.permutation(key_third, joined).astype(jnp.int32)


def level_of(key, dims, shards, smallest, high):
    def one(dim, blocks):
        steps = jax.random.uniform(jax.random.fold_in(jax.random.fold_in(key, 6), dim), (blocks,), jnp.float32, smallest / len(shards), high / len(shards))
        return jnp.repeat(jnp.exp(steps), dims[dim] // blocks).reshape((-1,) + (1,) * (len(dims) - dim - 1))

    level = one(*shards[0])
    for cut in shards[1:]:
        level = level * one(*cut)
    return level


def deal_out(key, own, number, rows, count, top, most, slope):
    order = jax.random.permutation(key, count)
    heavy_load, usual = portions_of(count, rows * top, most, slope, True), portions_of(count, rows * top, most, slope, False)
    places = jnp.arange(count)

    def named(tallies, offset_by):
        used = int((tallies > 0).sum())
        fixed = max(1, used // 4)
        moved = fixed + (places - fixed + offset_by * (used - fixed)) % max(1, count - fixed)
        return jnp.zeros((count,), jnp.int32).at[order[jnp.where(places < fixed, places, moved)]].set(jnp.asarray(tallies, jnp.int32))

    tallies = jnp.where(number % 4 == 0, named(heavy_load, number // 4), named(usual, number - number // 4 - 1))
    mixed = jax.random.permutation(jax.random.fold_in(own, 3), count)
    donor, sink = mixed[0:count // 2 * 2:2], mixed[1:count // 2 * 2:2]
    room = jnp.minimum(tallies[donor] - 1, most - tallies[sink]) // 2
    room = jnp.where((donor == order[0]) | (sink == order[0]) | (tallies[sink] == 0), 0, jnp.maximum(room, 0))
    moved = jax.random.randint(jax.random.fold_in(own, 4), (count // 2,), 0, 1 << 20) % (room + 1)
    tallies = tallies.at[donor].add(-moved).at[sink].add(moved)
    labels = jnp.searchsorted(jnp.cumsum(tallies), jnp.arange(rows * top), side="right").astype(jnp.int32)
    listing = labels.reshape(top, rows).T
    listing = listing[jax.random.permutation(jax.random.fold_in(own, 1), rows)]
    offset_by = jax.random.randint(jax.random.fold_in(own, 2), (rows, 1), 0, top)
    return jnp.take_along_axis(listing, (jnp.arange(top)[None, :] + offset_by) % top, axis=1)


def portions_of(amount, total, bound, lean, full):
    loads = [(1 << 20) // math.isqrt(grade ** lean) + 1 for grade in range(1, amount + 1)]
    largest = bound if full else min(bound, max(-(-total // amount), total * loads[0] // sum(loads)))
    least = 1 if total - largest >= amount - 1 else 0
    holding, rest = [largest] + [least] * (amount - 1), total - largest - least * (amount - 1)
    while rest > 0:
        movable = [i for i in range(1, amount) if holding[i] < largest] or [i for i in range(1, amount) if holding[i] < bound]
        whole, budget = sum([loads[i] for i in movable]), rest
        for i in movable:
            more = min(bound - holding[i], max(1, budget * loads[i] // whole), rest)
            holding[i] = holding[i] + more
            rest = rest - more
    return np.array(holding)


def noise(key, shape, scale, bound, cuts=(), kind=jnp.bfloat16):
    array = scale * jax.random.normal(key, shape, jnp.float32)
    if cuts:
        array = array * level_of(key, shape, cuts, -0.22, 0.18)
    return jnp.clip(array, -bound, bound).astype(kind)


def setup_inputs(seed: int = 0) -> dict:
    key_list = jax.random.split(jax.random.key(seed), 10)
    tokens = noise(key_list[0], (TOKENS, D), 1.0, 6.0, ((0, 256),))
    cotangent = noise(key_list[1], (TOKENS, D), 0.25, 1.5, ((0, 256),))
    routing_keys = jax.random.split(jax.random.fold_in(key_list[2], 1), TOKENS // TOK_DEV)
    routing_turns = jax.random.permutation(jax.random.fold_in(key_list[2], 3), TOKENS // TOK_DEV)
    routing = jax.vmap(lambda own, number: deal_out(jax.random.fold_in(key_list[2], 2), own, number, TOK_DEV, EXPERTS, TOPK, MOST, 2))(routing_keys, routing_turns).reshape((TOKENS, TOPK))
    gates = jnp.clip(0.19921875 + 0.80078125 * jax.random.uniform(key_list[3], (TOKENS, TOPK), jnp.float32) ** level_of(key_list[3], (TOKENS, TOPK), ((0, 256),), -0.2, 0.2), 0.19921875, 1.0).astype(jnp.bfloat16)
    new_place = draw_new_place(jax.random.fold_in(key_list[9], 71), 0)
    old_place = jax.random.permutation(key_list[5], EXPERTS).astype(jnp.int32)
    weights = noise(key_list[6], (3, EXPERTS, D, H), D ** -0.5, 0.125, ((2, 256),))
    first_moment = noise(key_list[7], (3, EXPERTS, D, H), 1.0, 6.0, ((2, 256),), jnp.float32)
    second_moment = jnp.clip(jnp.exp(math.log(20.0) - 3.6888795 * jax.random.uniform(key_list[8], (3, EXPERTS, D, H), jnp.float32) ** level_of(key_list[8], (3, EXPERTS, D, H), ((2, 256),), -0.2, 0.2)), 0.5, 20.0)
    return {"tokens": tokens, "cotangent": cotangent, "routing": routing, "gates": gates, "new_place": new_place, "old_place": old_place, "weights": weights, "first_moment": first_moment, "second_moment": second_moment}


beta_one = 0.9
beta_two = 0.95
learn_rate = 0.02
adam_step = 10.0
adam_eps = 1e-08

def expert_rows(inputs, upstream, gate_vals, stacked):
    first_pre = jnp.dot(inputs, stacked[0], preferred_element_type=jnp.float32)
    second_pre = jnp.dot(inputs, stacked[1], preferred_element_type=jnp.float32)
    back_proj = jnp.dot(upstream, stacked[2], preferred_element_type=jnp.float32)
    sigmoid_h = jax.nn.sigmoid(first_pre)
    activated = first_pre * sigmoid_h * second_pre
    gate_part = lax.optimization_barrier(jnp.sum(activated * back_proj, axis=1)).astype(jnp.bfloat16)
    weighted = gate_vals[:, None] * back_proj
    grad_second = (weighted * first_pre * sigmoid_h).astype(jnp.bfloat16)
    grad_first = (weighted * second_pre * sigmoid_h * (1.0 + first_pre * (1.0 - sigmoid_h))).astype(jnp.bfloat16)
    scaled_act = (gate_vals[:, None] * activated).astype(jnp.bfloat16)
    input_part = (jnp.dot(grad_first, stacked[0].T, preferred_element_type=jnp.float32) + jnp.dot(grad_second, stacked[1].T, preferred_element_type=jnp.float32)).astype(jnp.bfloat16)
    weight_grads = jnp.stack([jnp.dot(inputs.T, grad_first, preferred_element_type=jnp.float32), jnp.dot(inputs.T, grad_second, preferred_element_type=jnp.float32), jnp.dot(upstream.T, scaled_act, preferred_element_type=jnp.float32)])
    return (input_part, gate_part, weight_grads)

def adam_update(grad, stored, first, second):
    new_first = beta_one * first + (1.0 - beta_one) * grad
    new_second = beta_two * second + (1.0 - beta_two) * grad * grad
    first_hat = new_first / (1.0 - beta_one ** adam_step)
    second_hat = new_second / (1.0 - beta_two ** adam_step)
    updated = (stored.astype(jnp.float32) - learn_rate * first_hat / (jnp.sqrt(second_hat) + adam_eps)).astype(jnp.bfloat16)
    return (updated, new_first, new_second)

def reference(tokens, cotangent, routing, gates, new_place, old_place, weights, first_moment, second_moment):
    slot_count = N_EXPERT
    capacity = MOST
    total = TOKENS * TOPK
    block_count = N_DP * N_EXPERT
    per_block = TOK_DEV * TOPK
    expert_ids = jnp.arange(EXPERTS, dtype=jnp.int32)
    slot_ids = jnp.arange(slot_count, dtype=jnp.int32)
    place_hot = (new_place[:, None] == expert_ids[None, :]).astype(jnp.int32)
    replica_count = lax.optimization_barrier(jnp.sum(place_hot, axis=0))
    earlier = jnp.cumsum(place_hot, axis=0) - place_hot
    slot_rank = lax.optimization_barrier(jnp.sum(earlier * place_hot, axis=1))
    block_ids = jnp.arange(block_count, dtype=jnp.int32)
    source = block_ids % N_EXPERT
    wanted = source[:, None] % replica_count[None, :]
    chosen = place_hot[None, :, :] * (slot_rank[None, :, None] == wanted[:, None, :]).astype(jnp.int32)
    target_slot = lax.optimization_barrier(jnp.sum(chosen * slot_ids[None, :, None], axis=1))
    flat_experts = routing.reshape(block_count, per_block)
    assign_hot = (flat_experts[:, :, None] == expert_ids[None, None, :]).astype(jnp.int32)
    position = lax.optimization_barrier(jnp.sum((jnp.cumsum(assign_hot, axis=1) - assign_hot) * assign_hot, axis=2))
    slot_assign = lax.optimization_barrier(jnp.sum(assign_hot * target_slot[:, None, :], axis=2))
    dp_assign = jnp.broadcast_to((block_ids // N_EXPERT)[:, None], (block_count, per_block))
    column = source[:, None] * capacity + position
    assign_ids = jnp.arange(total, dtype=jnp.int32).reshape(block_count, per_block)
    table = jnp.full((N_DP, slot_count, slot_count * capacity), total, dtype=jnp.int32)
    table = table.at[dp_assign.reshape(-1).astype(jnp.int32), slot_assign.reshape(-1).astype(jnp.int32), column.reshape(-1).astype(jnp.int32)].set(assign_ids.reshape(-1))
    tok_pad = jnp.concatenate([tokens, jnp.zeros((1, D), tokens.dtype)], axis=0)
    cot_pad = jnp.concatenate([cotangent, jnp.zeros((1, D), cotangent.dtype)], axis=0)
    gate_pad = jnp.concatenate([gates.reshape(-1), jnp.zeros((1,), gates.dtype)], axis=0)
    inverse = jnp.zeros((EXPERTS,), jnp.int32).at[old_place].set(expert_ids)
    row_of_slot = inverse[new_place].astype(jnp.int32)

    def one_slot(carry, slot):
        input_rows, gate_rows_all = carry
        stacked = lax.dynamic_index_in_dim(weights, row_of_slot[slot], axis=1, keepdims=False)

        def one_row(running, data_row):
            picked = table[data_row, slot]
            token_index = picked // TOPK
            inputs = tok_pad[token_index]
            upstream = cot_pad[token_index]
            gate_vals = gate_pad[picked].astype(jnp.float32)
            input_part, gate_part, weight_grads = expert_rows(inputs, upstream, gate_vals, stacked)
            rounded = lax.optimization_barrier(weight_grads.astype(jnp.bfloat16))
            return (running + rounded.astype(jnp.float32), (input_part, gate_part))
        running, (parts, gate_parts) = lax.scan(one_row, jnp.zeros((3, D, H), jnp.float32), jnp.arange(N_DP, dtype=jnp.int32))
        picked_all = table[:, slot].reshape(-1)
        input_rows = input_rows.at[picked_all].set(parts.reshape(-1, D))
        gate_rows_all = gate_rows_all.at[picked_all].set(gate_parts.reshape(-1))
        return ((input_rows, gate_rows_all), running.astype(jnp.bfloat16))
    start = (jnp.zeros((total + 1, D), jnp.bfloat16), jnp.zeros((total + 1,), jnp.bfloat16))
    (input_rows, gate_rows_all), slot_grads = lax.scan(one_slot, start, slot_ids)
    input_rows = lax.optimization_barrier(input_rows)
    input_grad = lax.optimization_barrier(jnp.sum(input_rows[:total].reshape(TOKENS, TOPK, D).astype(jnp.float32), axis=1)).astype(jnp.bfloat16)
    gate_grad = gate_rows_all[:total].reshape(TOKENS, TOPK)
    slot_grads = lax.optimization_barrier(slot_grads)
    state_hot = (new_place[:, None] == old_place[None, :]).astype(jnp.float32)
    grad_state = jnp.einsum('sr,scdh->crdh', state_hot, slot_grads.astype(jnp.float32), precision=lax.Precision.HIGHEST)
    updated, new_first, new_second = adam_update(grad_state, weights, first_moment, second_moment)
    slot_weights = jnp.take(updated, row_of_slot, axis=1)
    return (input_grad, gate_grad, slot_weights, new_first, new_second)
```

```python
import jax
import jax.numpy as jnp
from jax import lax
from jax.sharding import PartitionSpec as P

beta_one = 0.9
beta_two = 0.95
learn_rate = 0.02
adam_step = 10.0
adam_eps = 1e-08


def adam_update(grad, stored, first, second):
    new_first = beta_one * first + (1.0 - beta_one) * grad
    new_second = beta_two * second + (1.0 - beta_two) * grad * grad
    first_hat = new_first / (1.0 - beta_one**adam_step)
    second_hat = new_second / (1.0 - beta_two**adam_step)
    updated = (
        stored.astype(jnp.float32) - learn_rate * first_hat / (jnp.sqrt(second_hat) + adam_eps)
    ).astype(jnp.bfloat16)
    return (updated, new_first, new_second)


def body(
    tokens, cotangent, routing, gates, new_place, old_place, weights, first_moment, second_moment
):
    tok_count, feature_width = tokens.shape
    top_count = routing.shape[1]
    expert_count = weights.shape[1]
    block_rows = weights.shape[2]
    hidden = weights.shape[3]
    slot_count = lax.axis_size("expert")
    capacity = 2 * tok_count * top_count // slot_count
    buffer_rows = slot_count * capacity
    source = lax.axis_index("expert")
    expert_ids = jnp.arange(expert_count, dtype=jnp.int32)
    slot_ids = jnp.arange(slot_count, dtype=jnp.int32)
    place_hot = (new_place[:, None] == expert_ids[None, :]).astype(jnp.int32)
    slot_state = (new_place[:, None] == old_place[None, :]).astype(jnp.bfloat16)

    outgoing = jnp.einsum(
        "se,cerh->scrh", slot_state, weights, preferred_element_type=jnp.float32
    ).astype(jnp.bfloat16)
    arrived = lax.all_to_all(outgoing, "expert", split_axis=0, concat_axis=0, tiled=True)
    gate_w, up_w, down_w = [
        lax.all_gather(
            arrived[:, c].reshape(slot_count * block_rows, hidden), "dp", axis=0, tiled=True
        )
        for c in range(3)
    ]

    replica_count = jnp.sum(place_hot, axis=0)
    earlier = jnp.cumsum(place_hot, axis=0) - place_hot
    slot_rank = jnp.sum(earlier * place_hot, axis=1)
    wanted = source % replica_count
    chosen = place_hot * (slot_rank[:, None] == wanted[None, :]).astype(jnp.int32)
    target_slot = jnp.sum(chosen * slot_ids[:, None], axis=0)
    flat_experts = routing.reshape(-1)
    assign_hot = (flat_experts[:, None] == expert_ids[None, :]).astype(jnp.int32)
    position = jnp.sum((jnp.cumsum(assign_hot, axis=0) - assign_hot) * assign_hot, axis=1)
    destination = jnp.sum(assign_hot * target_slot[None, :], axis=1) * capacity + position
    assign_dest = (
        destination[:, None] == jnp.arange(buffer_rows, dtype=jnp.int32)[None, :]
    ).astype(jnp.bfloat16)
    split_dest = assign_dest.reshape(tok_count, top_count, buffer_rows)
    token_dest = jnp.sum(split_dest, axis=1)
    gated_dest = jnp.sum(split_dest * gates[:, :, None], axis=1)

    def dispatch(where, rows):
        sent = jnp.einsum(
            "tb,td->bd", where, rows, preferred_element_type=jnp.float32
        ).astype(jnp.bfloat16)
        return lax.all_to_all(
            sent.reshape(slot_count, capacity, feature_width),
            "expert",
            split_axis=0,
            concat_axis=0,
            tiled=True,
        ).reshape(buffer_rows, feature_width)

    inputs = dispatch(token_dest, tokens)
    upstream = dispatch(gated_dest, cotangent)

    first_pre = jnp.dot(inputs, gate_w, preferred_element_type=jnp.float32)
    second_pre = jnp.dot(inputs, up_w, preferred_element_type=jnp.float32)
    weighted = jnp.dot(upstream, down_w, preferred_element_type=jnp.float32)
    sigmoid_h = jax.nn.sigmoid(first_pre)
    activated = first_pre * sigmoid_h * second_pre
    gate_part = jnp.sum(activated * weighted, axis=1).astype(jnp.bfloat16)
    grad_second = (weighted * first_pre * sigmoid_h).astype(jnp.bfloat16)
    grad_first = (weighted * second_pre * sigmoid_h * (1.0 + first_pre * (1.0 - sigmoid_h))).astype(
        jnp.bfloat16
    )
    act_low = activated.astype(jnp.bfloat16)

    def weight_grad(rows, units):
        grad = jnp.einsum("rd,rh->dh", rows, units, preferred_element_type=jnp.float32)
        return lax.psum_scatter(
            grad.astype(jnp.bfloat16), "dp", scatter_dimension=0, tiled=True
        ).reshape(slot_count, 1, block_rows, hidden)

    pieces = jnp.concatenate(
        [
            weight_grad(inputs, grad_first),
            weight_grad(inputs, grad_second),
            weight_grad(upstream, act_low),
        ],
        axis=1,
    )
    input_part = (
        jnp.einsum("rh,dh->rd", grad_first, gate_w, preferred_element_type=jnp.float32)
        + jnp.einsum("rh,dh->rd", grad_second, up_w, preferred_element_type=jnp.float32)
    ).astype(jnp.bfloat16)
    back_rows = lax.all_to_all(
        input_part.reshape(slot_count, capacity, feature_width),
        "expert",
        split_axis=0,
        concat_axis=0,
        tiled=True,
    )
    back_gates = lax.all_to_all(
        gate_part.reshape(slot_count, capacity),
        "expert",
        split_axis=0,
        concat_axis=0,
        tiled=True,
    )
    input_grad = jnp.einsum(
        "tb,bd->td",
        token_dest,
        back_rows.reshape(buffer_rows, feature_width),
        preferred_element_type=jnp.float32,
    ).astype(jnp.bfloat16)
    gate_sum = jnp.einsum(
        "ab,b->a", assign_dest, back_gates.reshape(-1), preferred_element_type=jnp.float32
    ).reshape(tok_count, top_count)
    gate_grad = (gate_sum / gates.astype(jnp.float32)).astype(jnp.bfloat16)

    returned = lax.all_to_all(pieces, "expert", split_axis=0, concat_axis=0, tiled=True)
    grad_state = jnp.einsum(
        "se,scrh->cerh", slot_state, returned, preferred_element_type=jnp.float32
    )
    updated, new_first, new_second = adam_update(grad_state, weights, first_moment, second_moment)
    leaving = jnp.einsum(
        "se,cerh->scrh", slot_state, updated, preferred_element_type=jnp.float32
    ).astype(jnp.bfloat16)
    landed = lax.all_to_all(leaving, "expert", split_axis=0, concat_axis=0, tiled=True)
    slot_weights = jnp.transpose(landed, (1, 0, 2, 3)).reshape(
        3, 1, slot_count * block_rows, hidden
    )
    return (input_grad, gate_grad, slot_weights, new_first, new_second)


def solution(mesh):
    placed = (
        P(("dp", "expert"), None),
        P(("dp", "expert"), None),
        P(("dp", "expert"), None),
        P(("dp", "expert"), None),
        P(),
        P(),
        P(None, None, ("dp", "expert"), None),
        P(None, None, ("dp", "expert"), None),
        P(None, None, ("dp", "expert"), None),
    )
    return jax.shard_map(
        body,
        mesh=mesh,
        in_specs=placed,
        out_specs=(
            P(("dp", "expert"), None),
            P(("dp", "expert"), None),
            P(None, "expert", "dp", None),
            P(None, None, ("dp", "expert"), None),
            P(None, None, ("dp", "expert"), None),
        ),
        check_vma=False,
    )
```

```python
import jax
import jax.numpy as jnp
from jax import lax
from jax.sharding import PartitionSpec as P

beta_one = 0.9
beta_two = 0.95
learn_rate = 0.02
adam_step = 10.0
adam_eps = 1e-08


def adam_update(grad, stored, first, second):
    new_first = beta_one * first + (1.0 - beta_one) * grad
    new_second = beta_two * second + (1.0 - beta_two) * grad * grad
    first_hat = new_first / (1.0 - beta_one**adam_step)
    second_hat = new_second / (1.0 - beta_two**adam_step)
    updated = (
        stored.astype(jnp.float32) - learn_rate * first_hat / (jnp.sqrt(second_hat) + adam_eps)
    ).astype(jnp.bfloat16)
    return (updated, new_first, new_second)


def body(
    tokens, cotangent, routing, gates, new_place, old_place, weights, first_moment, second_moment
):
    tok_count, feature_width = tokens.shape
    top_count = routing.shape[1]
    expert_count = weights.shape[1]
    block_rows = weights.shape[2]
    hidden = weights.shape[3]
    slot_count = lax.axis_size("expert")
    capacity = 2 * tok_count * top_count // slot_count
    buffer_rows = slot_count * capacity
    source = lax.axis_index("expert")
    expert_ids = jnp.arange(expert_count, dtype=jnp.int32)
    slot_ids = jnp.arange(slot_count, dtype=jnp.int32)
    place_hot = (new_place[:, None] == expert_ids[None, :]).astype(jnp.int32)
    slot_state = (new_place[:, None] == old_place[None, :]).astype(jnp.bfloat16)

    outgoing = jnp.einsum(
        "se,cerh->scrh", slot_state, weights, preferred_element_type=jnp.float32
    ).astype(jnp.bfloat16)
    arrived = lax.all_to_all(outgoing, "expert", split_axis=0, concat_axis=0, tiled=True)
    gate_w, up_w, down_w = [
        lax.all_gather(
            arrived[:, c].reshape(slot_count * block_rows, hidden), "dp", axis=0, tiled=True
        )
        for c in range(3)
    ]

    replica_count = jnp.sum(place_hot, axis=0)
    earlier = jnp.cumsum(place_hot, axis=0) - place_hot
    slot_rank = jnp.sum(earlier * place_hot, axis=1)
    wanted = source % replica_count
    chosen = place_hot * (slot_rank[:, None] == wanted[None, :]).astype(jnp.int32)
    target_slot = jnp.sum(chosen * slot_ids[:, None], axis=0)
    flat_experts = routing.reshape(-1)
    assign_hot = (flat_experts[:, None] == expert_ids[None, :]).astype(jnp.int32)
    position = jnp.sum((jnp.cumsum(assign_hot, axis=0) - assign_hot) * assign_hot, axis=1)
    destination = jnp.sum(assign_hot * target_slot[None, :], axis=1) * capacity + position
    assign_dest = (
        destination[:, None] == jnp.arange(buffer_rows, dtype=jnp.int32)[None, :]
    ).astype(jnp.bfloat16)
    split_dest = assign_dest.reshape(tok_count, top_count, buffer_rows)
    token_dest = jnp.sum(split_dest, axis=1)
    gated_dest = jnp.sum(split_dest * gates[:, :, None], axis=1)

    def dispatch(where, rows):
        sent = jnp.einsum(
            "tb,td->bd", where, rows, preferred_element_type=jnp.float32
        ).astype(jnp.bfloat16)
        return lax.all_to_all(
            sent.reshape(slot_count, capacity, feature_width),
            "expert",
            split_axis=0,
            concat_axis=0,
            tiled=True,
        ).reshape(buffer_rows, feature_width)

    inputs = dispatch(token_dest, tokens)
    upstream = dispatch(gated_dest, cotangent)

    first_pre = jnp.dot(inputs, gate_w, preferred_element_type=jnp.float32)
    second_pre = jnp.dot(inputs, up_w, preferred_element_type=jnp.float32)
    weighted = jnp.dot(upstream, down_w, preferred_element_type=jnp.float32)
    sigmoid_h = jax.nn.sigmoid(first_pre)
    activated = first_pre * sigmoid_h * second_pre
    gate_part = jnp.sum(activated * weighted, axis=1).astype(jnp.bfloat16)
    grad_second = (weighted * first_pre * sigmoid_h).astype(jnp.bfloat16)
    grad_first = (weighted * second_pre * sigmoid_h * (1.0 + first_pre * (1.0 - sigmoid_h))).astype(
        jnp.bfloat16
    )
    act_low = activated.astype(jnp.bfloat16)

    def weight_grad(rows, units):
        return jnp.einsum("rd,rh->dh", rows, units, preferred_element_type=jnp.float32).astype(
            jnp.bfloat16
        )

    weight_grads = jnp.stack(
        [
            weight_grad(inputs, grad_first),
            weight_grad(inputs, grad_second),
            weight_grad(upstream, act_low),
        ]
    )
    summed = lax.psum_scatter(weight_grads, "dp", scatter_dimension=1, tiled=True)
    pieces = jnp.transpose(summed.reshape(3, slot_count, block_rows, hidden), (1, 0, 2, 3))
    input_part = (
        jnp.einsum("rh,dh->rd", grad_first, gate_w, preferred_element_type=jnp.float32)
        + jnp.einsum("rh,dh->rd", grad_second, up_w, preferred_element_type=jnp.float32)
    ).astype(jnp.bfloat16)
    back_rows = lax.all_to_all(
        input_part.reshape(slot_count, capacity, feature_width),
        "expert",
        split_axis=0,
        concat_axis=0,
        tiled=True,
    )
    pieces, back_rows = lax.optimization_barrier((pieces, back_rows))
    back_gates = lax.all_to_all(
        gate_part.reshape(slot_count, capacity),
        "expert",
        split_axis=0,
        concat_axis=0,
        tiled=True,
    )
    input_grad = jnp.einsum(
        "tb,bd->td",
        token_dest,
        back_rows.reshape(buffer_rows, feature_width),
        preferred_element_type=jnp.float32,
    ).astype(jnp.bfloat16)
    gate_sum = jnp.einsum(
        "ab,b->a", assign_dest, back_gates.reshape(-1), preferred_element_type=jnp.float32
    ).reshape(tok_count, top_count)
    gate_grad = (gate_sum / gates.astype(jnp.float32)).astype(jnp.bfloat16)

    returned = lax.all_to_all(pieces, "expert", split_axis=0, concat_axis=0, tiled=True)
    grad_state = jnp.einsum(
        "se,scrh->cerh", slot_state, returned, preferred_element_type=jnp.float32
    )
    updated, new_first, new_second = adam_update(grad_state, weights, first_moment, second_moment)
    leaving = jnp.einsum(
        "se,cerh->scrh", slot_state, updated, preferred_element_type=jnp.float32
    ).astype(jnp.bfloat16)
    landed = lax.all_to_all(leaving, "expert", split_axis=0, concat_axis=0, tiled=True)
    slot_weights = jnp.transpose(landed, (1, 0, 2, 3)).reshape(
        3, 1, slot_count * block_rows, hidden
    )
    return (input_grad, gate_grad, slot_weights, new_first, new_second)


def solution(mesh):
    placed = (
        P(("dp", "expert"), None),
        P(("dp", "expert"), None),
        P(("dp", "expert"), None),
        P(("dp", "expert"), None),
        P(),
        P(),
        P(None, None, ("dp", "expert"), None),
        P(None, None, ("dp", "expert"), None),
        P(None, None, ("dp", "expert"), None),
    )
    return jax.shard_map(
        body,
        mesh=mesh,
        in_specs=placed,
        out_specs=(
            P(("dp", "expert"), None),
            P(("dp", "expert"), None),
            P(None, "expert", "dp", None),
            P(None, None, ("dp", "expert"), None),
            P(None, None, ("dp", "expert"), None),
        ),
        check_vma=False,
    )
```

```python
import jax
import jax.numpy as jnp
from jax import lax
from jax.experimental import pallas as pl
from jax.experimental.pallas import tpu as pltpu
from jax.sharding import PartitionSpec as P

beta_one = 0.9
beta_two = 0.95
learn_rate = 0.02
adam_step = 10.0
adam_eps = 1e-08


lane_count = 128
vmem_bytes = 56 * 1024 * 1024


def whole(shape):
    return pl.BlockSpec(shape, lambda i: (0,) * len(shape), pipeline_mode=pl.Buffered(1))


def grad_kernel(
    depth_steps, x_ref, y_ref, down_ref, first_ref, second_ref, dw_ref, units_ref, gate_ref
):
    step = pl.program_id(0)
    hidden = first_ref.shape[1]
    part = 256
    rows_depth = dw_ref.shape[1]

    @pl.when(step == 0)
    def _():
        total = jnp.zeros((first_ref.shape[0], 1), jnp.float32)
        for start in range(0, hidden, part):
            cols = pl.ds(start, part)
            weighted = jnp.dot(
                y_ref[...], down_ref[:, cols], preferred_element_type=jnp.float32
            )
            first_pre = first_ref[:, cols]
            second_pre = second_ref[:, cols]
            sigmoid_h = jax.nn.sigmoid(first_pre)
            gated = first_pre * sigmoid_h
            activated = gated * second_pre
            total = total + jnp.sum(activated * weighted, axis=1, keepdims=True)
            grad_first = weighted * second_pre * sigmoid_h * (1.0 + first_pre * (1.0 - sigmoid_h))
            units_ref[0, :, cols] = grad_first.astype(jnp.bfloat16)
            units_ref[1, :, cols] = (weighted * gated).astype(jnp.bfloat16)
            units_ref[2, :, cols] = activated.astype(jnp.bfloat16)
        gate_ref[...] = jnp.broadcast_to(total, gate_ref.shape).astype(jnp.bfloat16)

    which = step // depth_steps

    def product(rows):
        dw_ref[0] = lax.dot_general(
            rows, units_ref[which], (((0,), (0,)), ((), ())), preferred_element_type=jnp.float32
        ).astype(jnp.bfloat16)

    @pl.when(which < 2)
    def _():
        product(x_ref[...])

    @pl.when(which == 2)
    def _():
        place = pl.multiple_of(lax.rem(step, depth_steps) * rows_depth, rows_depth)
        product(y_ref[:, pl.ds(place, rows_depth)])


def unit_and_weight_grads(inputs, upstream, down_w, first_pre, second_pre):
    rows, width = inputs.shape
    hidden = down_w.shape[1]
    depth = 512
    steps = width // depth
    return pl.pallas_call(
        lambda *refs: grad_kernel(steps, *refs),
        grid=(3 * steps,),
        in_specs=[
            pl.BlockSpec((rows, depth), lambda i: (0, lax.rem(i, steps))),
            whole((rows, width)),
            whole((width, hidden)),
            whole((rows, hidden)),
            whole((rows, hidden)),
        ],
        out_specs=[
            pl.BlockSpec((1, depth, hidden), lambda i: (i // steps, lax.rem(i, steps), 0)),
            whole((3, rows, hidden)),
            whole((rows, lane_count)),
        ],
        out_shape=[
            jax.ShapeDtypeStruct((3, width, hidden), jnp.bfloat16),
            jax.ShapeDtypeStruct((3, rows, hidden), jnp.bfloat16),
            jax.ShapeDtypeStruct((rows, lane_count), jnp.bfloat16),
        ],
        compiler_params=pltpu.CompilerParams(vmem_limit_bytes=vmem_bytes),
        cost_estimate=pl.CostEstimate(
            flops=8 * rows * width * hidden, bytes_accessed=24_000_000, transcendentals=rows * hidden
        ),
    )(inputs, upstream, down_w, first_pre, second_pre)


def part_kernel(units_ref, gate_w_ref, up_w_ref, gate_ref, out_ref):
    width = gate_w_ref.shape[0]
    over_hidden = (((1,), (1,)), ((), ()))
    for start in range(0, width, 512):
        cols = pl.ds(start, 512)
        out_ref[:, cols] = (
            lax.dot_general(
                units_ref[0], gate_w_ref[cols], over_hidden, preferred_element_type=jnp.float32
            )
            + lax.dot_general(
                units_ref[1], up_w_ref[cols], over_hidden, preferred_element_type=jnp.float32
            )
        ).astype(jnp.bfloat16)
    out_ref[:, pl.ds(width, lane_count)] = gate_ref[...]


def input_parts(units, gate_w, up_w, gate_part):
    rows = units.shape[1]
    width, hidden = gate_w.shape
    block = 256
    return pl.pallas_call(
        part_kernel,
        grid=(rows // block,),
        in_specs=[
            pl.BlockSpec((2, block, hidden), lambda i: (0, i, 0)),
            whole((width, hidden)),
            whole((width, hidden)),
            pl.BlockSpec((block, lane_count), lambda i: (i, 0)),
        ],
        out_specs=pl.BlockSpec((block, width + lane_count), lambda i: (i, 0)),
        out_shape=jax.ShapeDtypeStruct((rows, width + lane_count), jnp.bfloat16),
        compiler_params=pltpu.CompilerParams(vmem_limit_bytes=vmem_bytes),
        cost_estimate=pl.CostEstimate(
            flops=4 * rows * width * hidden, bytes_accessed=10_000_000, transcendentals=0
        ),
    )(units, gate_w, up_w, gate_part)


def adam_update(grad, stored, first, second):
    new_first = beta_one * first + (1.0 - beta_one) * grad
    new_second = beta_two * second + (1.0 - beta_two) * grad * grad
    first_hat = new_first / (1.0 - beta_one**adam_step)
    second_hat = new_second / (1.0 - beta_two**adam_step)
    updated = (
        stored.astype(jnp.float32) - learn_rate * first_hat / (jnp.sqrt(second_hat) + adam_eps)
    ).astype(jnp.bfloat16)
    return (updated, new_first, new_second)


def body(
    tokens, cotangent, routing, gates, new_place, old_place, weights, first_moment, second_moment
):
    tok_count, feature_width = tokens.shape
    top_count = routing.shape[1]
    expert_count = weights.shape[1]
    block_rows = weights.shape[2]
    hidden = weights.shape[3]
    slot_count = lax.axis_size("expert")
    capacity = 2 * tok_count * top_count // slot_count
    buffer_rows = slot_count * capacity
    source = lax.axis_index("expert")
    expert_ids = jnp.arange(expert_count, dtype=jnp.int32)
    slot_ids = jnp.arange(slot_count, dtype=jnp.int32)
    place_hot = (new_place[:, None] == expert_ids[None, :]).astype(jnp.int32)
    slot_state = (new_place[:, None] == old_place[None, :]).astype(jnp.bfloat16)

    outgoing = jnp.einsum(
        "se,cerh->scrh", slot_state, weights, preferred_element_type=jnp.float32
    ).astype(jnp.bfloat16)
    arrived = lax.all_to_all(outgoing, "expert", split_axis=0, concat_axis=0, tiled=True)
    gate_w, up_w, down_w = [
        lax.all_gather(
            arrived[:, c].reshape(slot_count * block_rows, hidden), "dp", axis=0, tiled=True
        )
        for c in range(3)
    ]

    replica_count = jnp.sum(place_hot, axis=0)
    earlier = jnp.cumsum(place_hot, axis=0) - place_hot
    slot_rank = jnp.sum(earlier * place_hot, axis=1)
    wanted = source % replica_count
    chosen = place_hot * (slot_rank[:, None] == wanted[None, :]).astype(jnp.int32)
    target_slot = jnp.sum(chosen * slot_ids[:, None], axis=0)
    flat_experts = routing.reshape(-1)
    assign_hot = (flat_experts[:, None] == expert_ids[None, :]).astype(jnp.int32)
    position = jnp.sum((jnp.cumsum(assign_hot, axis=0) - assign_hot) * assign_hot, axis=1)
    destination = jnp.sum(assign_hot * target_slot[None, :], axis=1) * capacity + position
    assign_dest = (
        destination[:, None] == jnp.arange(buffer_rows, dtype=jnp.int32)[None, :]
    ).astype(jnp.bfloat16)
    split_dest = assign_dest.reshape(tok_count, top_count, buffer_rows)
    token_dest = jnp.sum(split_dest, axis=1)
    gated_dest = jnp.sum(split_dest * gates[:, :, None], axis=1)

    def dispatch(where, rows):
        sent = jnp.einsum(
            "tb,td->bd", where, rows, preferred_element_type=jnp.float32
        ).astype(jnp.bfloat16)
        return lax.all_to_all(
            sent.reshape(slot_count, capacity, feature_width),
            "expert",
            split_axis=0,
            concat_axis=0,
            tiled=True,
        ).reshape(buffer_rows, feature_width)

    inputs = dispatch(token_dest, tokens)
    upstream = dispatch(gated_dest, cotangent)

    first_pre = jnp.dot(inputs, gate_w, preferred_element_type=jnp.float32)
    second_pre = jnp.dot(inputs, up_w, preferred_element_type=jnp.float32)
    weight_grads, units, gate_part = unit_and_weight_grads(
        inputs, upstream, down_w, first_pre, second_pre
    )
    summed = lax.psum_scatter(weight_grads, "dp", scatter_dimension=1, tiled=True)
    pieces = jnp.transpose(summed.reshape(3, slot_count, block_rows, hidden), (1, 0, 2, 3))
    input_part = input_parts(units, gate_w, up_w, gate_part)
    back = lax.all_to_all(
        input_part.reshape(slot_count, capacity, feature_width + lane_count),
        "expert",
        split_axis=0,
        concat_axis=0,
        tiled=True,
    ).reshape(buffer_rows, feature_width + lane_count)
    pieces, back = lax.optimization_barrier((pieces, back))
    input_grad = jnp.einsum(
        "tb,bd->td", token_dest, back[:, :feature_width], preferred_element_type=jnp.float32
    ).astype(jnp.bfloat16)
    gate_sum = jnp.einsum(
        "ab,bl->al", assign_dest, back[:, feature_width:], preferred_element_type=jnp.float32
    )[:, 0].reshape(tok_count, top_count)
    gate_grad = (gate_sum / gates.astype(jnp.float32)).astype(jnp.bfloat16)

    returned = lax.all_to_all(pieces, "expert", split_axis=0, concat_axis=0, tiled=True)
    grad_state = jnp.einsum(
        "se,scrh->cerh", slot_state, returned, preferred_element_type=jnp.float32
    )
    updated, new_first, new_second = adam_update(grad_state, weights, first_moment, second_moment)
    leaving = jnp.einsum(
        "se,cerh->scrh", slot_state, updated, preferred_element_type=jnp.float32
    ).astype(jnp.bfloat16)
    landed = lax.all_to_all(leaving, "expert", split_axis=0, concat_axis=0, tiled=True)
    slot_weights = jnp.transpose(landed, (1, 0, 2, 3)).reshape(
        3, 1, slot_count * block_rows, hidden
    )
    return (input_grad, gate_grad, slot_weights, new_first, new_second)


def solution(mesh):
    placed = (
        P(("dp", "expert"), None),
        P(("dp", "expert"), None),
        P(("dp", "expert"), None),
        P(("dp", "expert"), None),
        P(),
        P(),
        P(None, None, ("dp", "expert"), None),
        P(None, None, ("dp", "expert"), None),
        P(None, None, ("dp", "expert"), None),
    )
    return jax.shard_map(
        body,
        mesh=mesh,
        in_specs=placed,
        out_specs=(
            P(("dp", "expert"), None),
            P(("dp", "expert"), None),
            P(None, "expert", "dp", None),
            P(None, None, ("dp", "expert"), None),
            P(None, None, ("dp", "expert"), None),
        ),
        check_vma=False,
    )
```

```python
import jax
import jax.numpy as jnp
from jax import lax
from jax.experimental import pallas as pl
from jax.experimental.pallas import tpu as pltpu
from jax.sharding import PartitionSpec as P

beta_one = 0.9
beta_two = 0.95
learn_rate = 0.02
adam_step = 10.0
adam_eps = 1e-08


lane_count = 128
vmem_bytes = 40 * 1024 * 1024


def whole(shape):
    return pl.BlockSpec(shape, lambda i: (0,) * len(shape), pipeline_mode=pl.Buffered(1))


def grad_kernel(
    u_steps,
    x_ref,
    y_ref,
    down_ref,
    first_hbm,
    second_hbm,
    dw_ref,
    units_ref,
    gate_ref,
    u_ref,
    first_ref,
    second_ref,
    sems,
):
    step = pl.program_id(0)
    rows, hidden = u_ref.shape
    part = 128
    fetch_first = pltpu.make_async_copy(first_hbm, first_ref, sems.at[0])
    fetch_second = pltpu.make_async_copy(second_hbm, second_ref, sems.at[1])

    @pl.when(step == 0)
    def _():
        fetch_first.start()
        fetch_second.start()
        u_ref[...] = jnp.dot(y_ref[...], down_ref[...], preferred_element_type=jnp.float32)

    @pl.when((step > 0) & (step < u_steps))
    def _():
        u_ref[...] += jnp.dot(y_ref[...], down_ref[...], preferred_element_type=jnp.float32)

    @pl.when(step == u_steps - 1)
    def _():
        fetch_first.wait()
        fetch_second.wait()
        for start in range(0, rows, part):
            span = pl.ds(start, part)
            weighted = u_ref[span]
            first_pre = first_ref[span]
            second_pre = second_ref[span]
            sigmoid_h = jax.nn.sigmoid(first_pre)
            gated = first_pre * sigmoid_h
            activated = gated * second_pre
            total = jnp.sum(activated * weighted, axis=1, keepdims=True)
            grad_first = weighted * second_pre * sigmoid_h * (1.0 + first_pre * (1.0 - sigmoid_h))
            units_ref[span, :hidden] = grad_first.astype(jnp.bfloat16)
            units_ref[span, hidden : 2 * hidden] = (weighted * gated).astype(jnp.bfloat16)
            units_ref[span, 2 * hidden :] = activated.astype(jnp.bfloat16)
            gate_ref[span] = jnp.broadcast_to(total, (part, lane_count)).astype(jnp.bfloat16)

    @pl.when(step >= u_steps)
    def _():
        both = jnp.dot(
            x_ref[...].T, units_ref[:, : 2 * hidden], preferred_element_type=jnp.float32
        ).astype(jnp.bfloat16)
        dw_ref[0] = both[:, :hidden]
        dw_ref[1] = both[:, hidden:]
        dw_ref[2] = jnp.dot(
            y_ref[...].T, units_ref[:, 2 * hidden :], preferred_element_type=jnp.float32
        ).astype(jnp.bfloat16)


def unit_and_weight_grads(inputs, upstream, down_w, first_pre, second_pre):
    rows, width = inputs.shape
    hidden = down_w.shape[1]
    depth = 512
    steps = width // depth
    return pl.pallas_call(
        lambda *refs: grad_kernel(steps, *refs),
        grid=(2 * steps,),
        in_specs=[
            pl.BlockSpec((rows, depth), lambda i: (0, jnp.maximum(i - steps, 0))),
            pl.BlockSpec((rows, depth), lambda i: (0, lax.rem(i, steps))),
            pl.BlockSpec((depth, hidden), lambda i: (jnp.minimum(i, steps - 1), 0)),
            pl.BlockSpec(memory_space=pl.ANY),
            pl.BlockSpec(memory_space=pl.ANY),
        ],
        out_specs=[
            pl.BlockSpec((3, depth, hidden), lambda i: (0, jnp.maximum(i - steps, 0), 0)),
            whole((rows, 3 * hidden)),
            whole((rows, lane_count)),
        ],
        out_shape=[
            jax.ShapeDtypeStruct((3, width, hidden), jnp.bfloat16),
            jax.ShapeDtypeStruct((rows, 3 * hidden), jnp.bfloat16),
            jax.ShapeDtypeStruct((rows, lane_count), jnp.bfloat16),
        ],
        scratch_shapes=[
            pltpu.VMEM((rows, hidden), jnp.float32),
            pltpu.VMEM((rows, hidden), jnp.float32),
            pltpu.VMEM((rows, hidden), jnp.float32),
            pltpu.SemaphoreType.DMA((2,)),
        ],
        compiler_params=pltpu.CompilerParams(vmem_limit_bytes=vmem_bytes),
        cost_estimate=pl.CostEstimate(
            flops=8 * rows * width * hidden, bytes_accessed=24_000_000, transcendentals=rows * hidden
        ),
    )(inputs, upstream, down_w, first_pre, second_pre)


def part_kernel(units_ref, gate_w_ref, up_w_ref, gate_ref, out_ref):
    step = pl.program_id(0)
    depth, hidden = gate_w_ref.shape
    over_hidden = (((1,), (1,)), ((), ()))

    @pl.when(step == 0)
    def _():
        out_ref[:, pl.ds(out_ref.shape[1] - lane_count, lane_count)] = gate_ref[...]

    out_ref[:, pl.ds(pl.multiple_of(step * depth, depth), depth)] = (
        lax.dot_general(
            units_ref[:, :hidden], gate_w_ref[...], over_hidden, preferred_element_type=jnp.float32
        )
        + lax.dot_general(
            units_ref[:, hidden : 2 * hidden],
            up_w_ref[...],
            over_hidden,
            preferred_element_type=jnp.float32,
        )
    ).astype(jnp.bfloat16)


def input_parts(units, gate_w, up_w, gate_part):
    rows = units.shape[0]
    width, hidden = gate_w.shape
    depth = 512
    return pl.pallas_call(
        part_kernel,
        grid=(width // depth,),
        in_specs=[
            whole((rows, 3 * hidden)),
            pl.BlockSpec((depth, hidden), lambda i: (i, 0)),
            pl.BlockSpec((depth, hidden), lambda i: (i, 0)),
            whole((rows, lane_count)),
        ],
        out_specs=whole((rows, width + lane_count)),
        out_shape=jax.ShapeDtypeStruct((rows, width + lane_count), jnp.bfloat16),
        compiler_params=pltpu.CompilerParams(vmem_limit_bytes=vmem_bytes),
        cost_estimate=pl.CostEstimate(
            flops=4 * rows * width * hidden, bytes_accessed=10_000_000, transcendentals=0
        ),
    )(units, gate_w, up_w, gate_part)


def adam_update(grad, stored, first, second):
    new_first = beta_one * first + (1.0 - beta_one) * grad
    new_second = beta_two * second + (1.0 - beta_two) * grad * grad
    first_hat = new_first / (1.0 - beta_one**adam_step)
    second_hat = new_second / (1.0 - beta_two**adam_step)
    updated = (
        stored.astype(jnp.float32) - learn_rate * first_hat / (jnp.sqrt(second_hat) + adam_eps)
    ).astype(jnp.bfloat16)
    return (updated, new_first, new_second)


def body(
    tokens, cotangent, routing, gates, new_place, old_place, weights, first_moment, second_moment
):
    tok_count, feature_width = tokens.shape
    top_count = routing.shape[1]
    expert_count = weights.shape[1]
    block_rows = weights.shape[2]
    hidden = weights.shape[3]
    slot_count = lax.axis_size("expert")
    capacity = 2 * tok_count * top_count // slot_count
    buffer_rows = slot_count * capacity
    source = lax.axis_index("expert")
    expert_ids = jnp.arange(expert_count, dtype=jnp.int32)
    slot_ids = jnp.arange(slot_count, dtype=jnp.int32)
    place_hot = (new_place[:, None] == expert_ids[None, :]).astype(jnp.int32)
    slot_state = (new_place[:, None] == old_place[None, :]).astype(jnp.bfloat16)

    outgoing = jnp.einsum(
        "se,cerh->scrh", slot_state, weights, preferred_element_type=jnp.float32
    ).astype(jnp.bfloat16)
    arrived = lax.all_to_all(outgoing, "expert", split_axis=0, concat_axis=0, tiled=True)

    replica_count = jnp.sum(place_hot, axis=0)
    earlier = jnp.cumsum(place_hot, axis=0) - place_hot
    slot_rank = jnp.sum(earlier * place_hot, axis=1)
    wanted = source % replica_count
    chosen = place_hot * (slot_rank[:, None] == wanted[None, :]).astype(jnp.int32)
    target_slot = jnp.sum(chosen * slot_ids[:, None], axis=0)
    flat_experts = routing.reshape(-1)
    assign_hot = (flat_experts[:, None] == expert_ids[None, :]).astype(jnp.int32)
    position = jnp.sum((jnp.cumsum(assign_hot, axis=0) - assign_hot) * assign_hot, axis=1)
    destination = jnp.sum(assign_hot * target_slot[None, :], axis=1) * capacity + position
    assign_dest = (
        destination[:, None] == jnp.arange(buffer_rows, dtype=jnp.int32)[None, :]
    ).astype(jnp.bfloat16)
    split_dest = assign_dest.reshape(tok_count, top_count, buffer_rows)
    token_dest = jnp.sum(split_dest, axis=1)
    gated_dest = jnp.sum(split_dest * gates[:, :, None], axis=1)

    def pack(where, rows):
        return (
            jnp.einsum("tb,td->bd", where, rows, preferred_element_type=jnp.float32)
            .astype(jnp.bfloat16)
            .reshape(slot_count, capacity, feature_width)
        )

    def dispatch(packed):
        return lax.all_to_all(packed, "expert", split_axis=0, concat_axis=0, tiled=True).reshape(
            buffer_rows, feature_width
        )

    arrived, packed_tokens, packed_upstream = lax.optimization_barrier(
        (arrived, pack(token_dest, tokens), pack(gated_dest, cotangent))
    )
    gate_w, up_w, down_w = [
        lax.all_gather(
            arrived[:, c].reshape(slot_count * block_rows, hidden), "dp", axis=0, tiled=True
        )
        for c in range(3)
    ]
    inputs = dispatch(packed_tokens)
    upstream = dispatch(packed_upstream)

    first_pre = jnp.dot(inputs, gate_w, preferred_element_type=jnp.float32)
    second_pre = jnp.dot(inputs, up_w, preferred_element_type=jnp.float32)
    weight_grads, units, gate_part = unit_and_weight_grads(
        inputs, upstream, down_w, first_pre, second_pre
    )
    summed = lax.psum_scatter(weight_grads, "dp", scatter_dimension=1, tiled=True)
    pieces = jnp.transpose(summed.reshape(3, slot_count, block_rows, hidden), (1, 0, 2, 3))
    input_part = input_parts(units, gate_w, up_w, gate_part)
    back = lax.all_to_all(
        input_part.reshape(slot_count, capacity, feature_width + lane_count),
        "expert",
        split_axis=0,
        concat_axis=0,
        tiled=True,
    ).reshape(buffer_rows, feature_width + lane_count)
    pieces, back = lax.optimization_barrier((pieces, back))
    input_grad = jnp.einsum(
        "tb,bd->td", token_dest, back[:, :feature_width], preferred_element_type=jnp.float32
    ).astype(jnp.bfloat16)
    gate_sum = jnp.einsum(
        "ab,bl->al", assign_dest, back[:, feature_width:], preferred_element_type=jnp.float32
    )[:, 0].reshape(tok_count, top_count)
    gate_grad = (gate_sum / gates.astype(jnp.float32)).astype(jnp.bfloat16)

    returned = lax.all_to_all(pieces, "expert", split_axis=0, concat_axis=0, tiled=True)
    grad_state = jnp.einsum(
        "se,scrh->cerh", slot_state, returned, preferred_element_type=jnp.float32
    )
    updated, new_first, new_second = adam_update(grad_state, weights, first_moment, second_moment)
    leaving = jnp.einsum(
        "se,cerh->scrh", slot_state, updated, preferred_element_type=jnp.float32
    ).astype(jnp.bfloat16)
    landed = lax.all_to_all(leaving, "expert", split_axis=0, concat_axis=0, tiled=True)
    slot_weights = jnp.transpose(landed, (1, 0, 2, 3)).reshape(
        3, 1, slot_count * block_rows, hidden
    )
    return (input_grad, gate_grad, slot_weights, new_first, new_second)


def solution(mesh):
    placed = (
        P(("dp", "expert"), None),
        P(("dp", "expert"), None),
        P(("dp", "expert"), None),
        P(("dp", "expert"), None),
        P(),
        P(),
        P(None, None, ("dp", "expert"), None),
        P(None, None, ("dp", "expert"), None),
        P(None, None, ("dp", "expert"), None),
    )
    return jax.shard_map(
        body,
        mesh=mesh,
        in_specs=placed,
        out_specs=(
            P(("dp", "expert"), None),
            P(("dp", "expert"), None),
            P(None, "expert", "dp", None),
            P(None, None, ("dp", "expert"), None),
            P(None, None, ("dp", "expert"), None),
        ),
        check_vma=False,
    )
```

```python
import jax
import jax.numpy as jnp
from jax import lax
from jax.experimental import pallas as pl
from jax.experimental.pallas import tpu as pltpu
from jax.sharding import PartitionSpec as P

beta_one = 0.9
beta_two = 0.95
learn_rate = 0.02
adam_step = 10.0
adam_eps = 1e-08


lane_count = 128
vmem_bytes = 60 * 1024 * 1024


def whole(shape):
    return pl.BlockSpec(shape, lambda i: (0,) * len(shape), pipeline_mode=pl.Buffered(1))


def grad_kernel(
    u_steps,
    x_ref,
    y_ref,
    down_ref,
    first_hbm,
    second_hbm,
    dw_ref,
    units_ref,
    gate_ref,
    u_ref,
    first_ref,
    second_ref,
    sems,
):
    step = pl.program_id(0)
    rows, hidden = u_ref.shape
    part = 128
    fetch_first = pltpu.make_async_copy(first_hbm, first_ref, sems.at[0])
    fetch_second = pltpu.make_async_copy(second_hbm, second_ref, sems.at[1])

    @pl.when(step == 0)
    def _():
        fetch_first.start()
        fetch_second.start()
        u_ref[...] = jnp.dot(y_ref[...], down_ref[...], preferred_element_type=jnp.float32)

    @pl.when((step > 0) & (step < u_steps))
    def _():
        u_ref[...] += jnp.dot(y_ref[...], down_ref[...], preferred_element_type=jnp.float32)

    @pl.when(step == u_steps - 1)
    def _():
        fetch_first.wait()
        fetch_second.wait()
        for start in range(0, rows, part):
            span = pl.ds(start, part)
            weighted = u_ref[span]
            first_pre = first_ref[span]
            second_pre = second_ref[span]
            sigmoid_h = jax.nn.sigmoid(first_pre)
            gated = first_pre * sigmoid_h
            activated = gated * second_pre
            total = jnp.sum(activated * weighted, axis=1, keepdims=True)
            grad_first = weighted * second_pre * sigmoid_h * (1.0 + first_pre * (1.0 - sigmoid_h))
            units_ref[span, :hidden] = grad_first.astype(jnp.bfloat16)
            units_ref[span, hidden : 2 * hidden] = (weighted * gated).astype(jnp.bfloat16)
            units_ref[span, 2 * hidden :] = activated.astype(jnp.bfloat16)
            gate_ref[span] = jnp.broadcast_to(total, (part, lane_count)).astype(jnp.bfloat16)

    @pl.when(step >= u_steps)
    def _():
        both = jnp.dot(
            x_ref[...].T, units_ref[:, : 2 * hidden], preferred_element_type=jnp.float32
        ).astype(jnp.bfloat16)
        dw_ref[0] = both[:, :hidden]
        dw_ref[1] = both[:, hidden:]
        dw_ref[2] = jnp.dot(
            y_ref[...].T, units_ref[:, 2 * hidden :], preferred_element_type=jnp.float32
        ).astype(jnp.bfloat16)


def unit_and_weight_grads(inputs, upstream, down_w, first_pre, second_pre):
    rows, width = inputs.shape
    hidden = down_w.shape[1]
    depth = 512
    steps = width // depth
    return pl.pallas_call(
        lambda *refs: grad_kernel(steps, *refs),
        grid=(2 * steps,),
        in_specs=[
            pl.BlockSpec((rows, depth), lambda i: (0, jnp.maximum(i - steps, 0))),
            pl.BlockSpec((rows, depth), lambda i: (0, lax.rem(i, steps))),
            pl.BlockSpec((depth, hidden), lambda i: (jnp.minimum(i, steps - 1), 0)),
            pl.BlockSpec(memory_space=pl.ANY),
            pl.BlockSpec(memory_space=pl.ANY),
        ],
        out_specs=[
            pl.BlockSpec((3, depth, hidden), lambda i: (0, jnp.maximum(i - steps, 0), 0)),
            whole((rows, 3 * hidden)),
            whole((rows, lane_count)),
        ],
        out_shape=[
            jax.ShapeDtypeStruct((3, width, hidden), jnp.bfloat16),
            jax.ShapeDtypeStruct((rows, 3 * hidden), jnp.bfloat16),
            jax.ShapeDtypeStruct((rows, lane_count), jnp.bfloat16),
        ],
        scratch_shapes=[
            pltpu.VMEM((rows, hidden), jnp.float32),
            pltpu.VMEM((rows, hidden), jnp.float32),
            pltpu.VMEM((rows, hidden), jnp.float32),
            pltpu.SemaphoreType.DMA((2,)),
        ],
        compiler_params=pltpu.CompilerParams(vmem_limit_bytes=vmem_bytes),
        cost_estimate=pl.CostEstimate(
            flops=8 * rows * width * hidden, bytes_accessed=24_000_000, transcendentals=rows * hidden
        ),
    )(inputs, upstream, down_w, first_pre, second_pre)


def part_kernel(units_ref, gate_w_ref, up_w_ref, gate_ref, out_ref):
    step = pl.program_id(0)
    depth, hidden = gate_w_ref.shape
    over_hidden = (((1,), (1,)), ((), ()))

    @pl.when(step == 0)
    def _():
        out_ref[:, pl.ds(out_ref.shape[1] - lane_count, lane_count)] = gate_ref[...]

    out_ref[:, pl.ds(pl.multiple_of(step * depth, depth), depth)] = (
        lax.dot_general(
            units_ref[:, :hidden], gate_w_ref[...], over_hidden, preferred_element_type=jnp.float32
        )
        + lax.dot_general(
            units_ref[:, hidden : 2 * hidden],
            up_w_ref[...],
            over_hidden,
            preferred_element_type=jnp.float32,
        )
    ).astype(jnp.bfloat16)


def input_parts(units, gate_w, up_w, gate_part):
    rows = units.shape[0]
    width, hidden = gate_w.shape
    depth = 512
    return pl.pallas_call(
        part_kernel,
        grid=(width // depth,),
        in_specs=[
            whole((rows, 3 * hidden)),
            pl.BlockSpec((depth, hidden), lambda i: (i, 0)),
            pl.BlockSpec((depth, hidden), lambda i: (i, 0)),
            whole((rows, lane_count)),
        ],
        out_specs=whole((rows, width + lane_count)),
        out_shape=jax.ShapeDtypeStruct((rows, width + lane_count), jnp.bfloat16),
        compiler_params=pltpu.CompilerParams(vmem_limit_bytes=vmem_bytes),
        cost_estimate=pl.CostEstimate(
            flops=4 * rows * width * hidden, bytes_accessed=10_000_000, transcendentals=0
        ),
    )(units, gate_w, up_w, gate_part)


def adam_update(grad, stored, first, second):
    new_first = beta_one * first + (1.0 - beta_one) * grad
    new_second = beta_two * second + (1.0 - beta_two) * grad * grad
    first_hat = new_first / (1.0 - beta_one**adam_step)
    second_hat = new_second / (1.0 - beta_two**adam_step)
    updated = (
        stored.astype(jnp.float32) - learn_rate * first_hat / (jnp.sqrt(second_hat) + adam_eps)
    ).astype(jnp.bfloat16)
    return (updated, new_first, new_second)


def body(
    tokens, cotangent, routing, gates, new_place, old_place, weights, first_moment, second_moment
):
    tok_count, feature_width = tokens.shape
    top_count = routing.shape[1]
    expert_count = weights.shape[1]
    block_rows = weights.shape[2]
    hidden = weights.shape[3]
    slot_count = lax.axis_size("expert")
    capacity = 2 * tok_count * top_count // slot_count
    buffer_rows = slot_count * capacity
    source = lax.axis_index("expert")
    expert_ids = jnp.arange(expert_count, dtype=jnp.int32)
    slot_ids = jnp.arange(slot_count, dtype=jnp.int32)
    place_hot = (new_place[:, None] == expert_ids[None, :]).astype(jnp.int32)
    slot_state = (new_place[:, None] == old_place[None, :]).astype(jnp.bfloat16)

    outgoing = jnp.einsum(
        "se,cerh->scrh", slot_state, weights, preferred_element_type=jnp.float32
    ).astype(jnp.bfloat16)
    arrived = lax.all_to_all(outgoing, "expert", split_axis=0, concat_axis=0, tiled=True)

    replica_count = jnp.sum(place_hot, axis=0)
    earlier = jnp.cumsum(place_hot, axis=0) - place_hot
    slot_rank = jnp.sum(earlier * place_hot, axis=1)
    wanted = source % replica_count
    chosen = place_hot * (slot_rank[:, None] == wanted[None, :]).astype(jnp.int32)
    target_slot = jnp.sum(chosen * slot_ids[:, None], axis=0)
    flat_experts = routing.reshape(-1)
    assign_hot = (flat_experts[:, None] == expert_ids[None, :]).astype(jnp.int32)
    position = jnp.sum((jnp.cumsum(assign_hot, axis=0) - assign_hot) * assign_hot, axis=1)
    destination = jnp.sum(assign_hot * target_slot[None, :], axis=1) * capacity + position
    assign_dest = (
        destination[:, None] == jnp.arange(buffer_rows, dtype=jnp.int32)[None, :]
    ).astype(jnp.bfloat16)
    split_dest = assign_dest.reshape(tok_count, top_count, buffer_rows)
    token_dest = jnp.sum(split_dest, axis=1)
    gated_dest = jnp.sum(split_dest * gates[:, :, None], axis=1)

    def pack(where, rows):
        return (
            jnp.einsum("tb,td->bd", where, rows, preferred_element_type=jnp.float32)
            .astype(jnp.bfloat16)
            .reshape(slot_count, capacity, feature_width)
        )

    def dispatch(packed):
        return lax.all_to_all(packed, "expert", split_axis=0, concat_axis=0, tiled=True).reshape(
            buffer_rows, feature_width
        )

    arrived, packed_tokens, packed_upstream = lax.optimization_barrier(
        (arrived, pack(token_dest, tokens), pack(gated_dest, cotangent))
    )
    gate_w, up_w, down_w = [
        lax.all_gather(
            arrived[:, c].reshape(slot_count * block_rows, hidden), "dp", axis=0, tiled=True
        )
        for c in range(3)
    ]
    inputs = dispatch(packed_tokens)
    upstream = dispatch(packed_upstream)

    first_pre = jnp.dot(inputs, gate_w, preferred_element_type=jnp.float32)
    second_pre = jnp.dot(inputs, up_w, preferred_element_type=jnp.float32)
    weight_grads, units, gate_part = unit_and_weight_grads(
        inputs, upstream, down_w, first_pre, second_pre
    )
    summed = lax.psum_scatter(weight_grads, "dp", scatter_dimension=1, tiled=True)
    pieces = jnp.transpose(summed.reshape(3, slot_count, block_rows, hidden), (1, 0, 2, 3))
    input_part = input_parts(units, gate_w, up_w, gate_part)
    back = lax.all_to_all(
        input_part.reshape(slot_count, capacity, feature_width + lane_count),
        "expert",
        split_axis=0,
        concat_axis=0,
        tiled=True,
    ).reshape(buffer_rows, feature_width + lane_count)
    pieces, back = lax.optimization_barrier((pieces, back))
    input_grad = jnp.einsum(
        "tb,bd->td", token_dest, back[:, :feature_width], preferred_element_type=jnp.float32
    ).astype(jnp.bfloat16)
    gate_sum = jnp.einsum(
        "ab,bl->al", assign_dest, back[:, feature_width:], preferred_element_type=jnp.float32
    )[:, 0].reshape(tok_count, top_count)
    gate_grad = (gate_sum / gates.astype(jnp.float32)).astype(jnp.bfloat16)

    returned = lax.all_to_all(pieces, "expert", split_axis=0, concat_axis=0, tiled=True)
    grad_state = jnp.einsum(
        "se,scrh->cerh", slot_state, returned, preferred_element_type=jnp.float32
    )
    updated, new_first, new_second = adam_update(grad_state, weights, first_moment, second_moment)
    leaving = jnp.einsum(
        "se,cerh->scrh", slot_state, updated, preferred_element_type=jnp.float32
    ).astype(jnp.bfloat16)
    landed = lax.all_to_all(leaving, "expert", split_axis=0, concat_axis=0, tiled=True)
    slot_weights = jnp.transpose(landed, (1, 0, 2, 3)).reshape(
        3, 1, slot_count * block_rows, hidden
    )
    return (input_grad, gate_grad, slot_weights, new_first, new_second)


def solution(mesh):
    placed = (
        P(("dp", "expert"), None),
        P(("dp", "expert"), None),
        P(("dp", "expert"), None),
        P(("dp", "expert"), None),
        P(),
        P(),
        P(None, None, ("dp", "expert"), None),
        P(None, None, ("dp", "expert"), None),
        P(None, None, ("dp", "expert"), None),
    )
    return jax.shard_map(
        body,
        mesh=mesh,
        in_specs=placed,
        out_specs=(
            P(("dp", "expert"), None),
            P(("dp", "expert"), None),
            P(None, "expert", "dp", None),
            P(None, None, ("dp", "expert"), None),
            P(None, None, ("dp", "expert"), None),
        ),
        check_vma=False,
    )
```

```python
import jax
import jax.numpy as jnp
from jax import lax
from jax.experimental import pallas as pl
from jax.experimental.pallas import tpu as pltpu
from jax.sharding import PartitionSpec as P

beta_one = 0.9
beta_two = 0.95
learn_rate = 0.02
adam_step = 10.0
adam_eps = 1e-08


lane_count = 128
vmem_bytes = 60 * 1024 * 1024


def whole(shape):
    return pl.BlockSpec(shape, lambda i: (0,) * len(shape), pipeline_mode=pl.Buffered(1))


def flat_rows(ref):
    return ref[...].reshape(-1, ref.shape[-1])


def grad_kernel(
    steps,
    x_ref,
    y_ref,
    gate_w_ref,
    up_w_ref,
    down_w_ref,
    dw_ref,
    units_ref,
    gate_ref,
    first_ref,
    second_ref,
    u_ref,
):
    step = pl.program_id(0)
    rows, hidden = u_ref.shape
    part = 128
    products = ((first_ref, x_ref, gate_w_ref), (second_ref, x_ref, up_w_ref), (u_ref, y_ref, down_w_ref))

    @pl.when(step == 0)
    def _():
        for total, left, right in products:
            total[...] = jnp.dot(
                flat_rows(left), flat_rows(right), preferred_element_type=jnp.float32
            )

    @pl.when((step > 0) & (step < steps))
    def _():
        for total, left, right in products:
            total[...] += jnp.dot(
                flat_rows(left), flat_rows(right), preferred_element_type=jnp.float32
            )

    @pl.when(step == steps - 1)
    def _():
        for start in range(0, rows, part):
            span = pl.ds(start, part)
            weighted = u_ref[span]
            first_pre = first_ref[span]
            second_pre = second_ref[span]
            sigmoid_h = jax.nn.sigmoid(first_pre)
            gated = first_pre * sigmoid_h
            activated = gated * second_pre
            total = jnp.sum(activated * weighted, axis=1, keepdims=True)
            grad_first = weighted * second_pre * sigmoid_h * (1.0 + first_pre * (1.0 - sigmoid_h))
            units_ref[span, :hidden] = grad_first.astype(jnp.bfloat16)
            units_ref[span, hidden : 2 * hidden] = (weighted * gated).astype(jnp.bfloat16)
            units_ref[span, 2 * hidden :] = activated.astype(jnp.bfloat16)
            gate_ref[span] = jnp.broadcast_to(total, (part, lane_count)).astype(jnp.bfloat16)

    @pl.when(step >= steps)
    def _():
        both = jnp.dot(
            flat_rows(x_ref).T, units_ref[:, : 2 * hidden], preferred_element_type=jnp.float32
        ).astype(jnp.bfloat16)
        dw_ref[0] = both[:, :hidden]
        dw_ref[1] = both[:, hidden:]
        dw_ref[2] = jnp.dot(
            flat_rows(y_ref).T, units_ref[:, 2 * hidden :], preferred_element_type=jnp.float32
        ).astype(jnp.bfloat16)


def weight_block(stacked, matrix, depth, block_of):
    _, _, rows, hidden = stacked.shape
    return pl.BlockSpec((depth // rows, 1, rows, hidden), lambda i: (block_of(i), matrix, 0, 0))


def unit_and_weight_grads(received, stacked):
    sources, _, capacity, width = received.shape
    hidden = stacked.shape[3]
    rows = sources * capacity
    depth = 512
    steps = width // depth

    def row_block(which):
        return pl.BlockSpec(
            (sources, 1, capacity, depth), lambda i: (0, which, 0, lax.rem(i, steps))
        )

    return pl.pallas_call(
        lambda *refs: grad_kernel(steps, *refs),
        grid=(2 * steps,),
        in_specs=[row_block(0), row_block(1)]
        + [weight_block(stacked, c, depth, lambda i: jnp.minimum(i, steps - 1)) for c in range(3)],
        out_specs=[
            pl.BlockSpec((3, depth, hidden), lambda i: (0, jnp.maximum(i - steps, 0), 0)),
            whole((rows, 3 * hidden)),
            whole((rows, lane_count)),
        ],
        out_shape=[
            jax.ShapeDtypeStruct((3, width, hidden), jnp.bfloat16),
            jax.ShapeDtypeStruct((rows, 3 * hidden), jnp.bfloat16),
            jax.ShapeDtypeStruct((rows, lane_count), jnp.bfloat16),
        ],
        scratch_shapes=[pltpu.VMEM((rows, hidden), jnp.float32)] * 3,
        compiler_params=pltpu.CompilerParams(vmem_limit_bytes=vmem_bytes),
        cost_estimate=pl.CostEstimate(
            flops=12 * rows * width * hidden,
            bytes_accessed=30_000_000,
            transcendentals=rows * hidden,
        ),
    )(received, received, stacked, stacked, stacked)


def part_kernel(units_ref, gate_w_ref, up_w_ref, gate_ref, out_ref):
    step = pl.program_id(0)
    hidden = gate_w_ref.shape[-1]
    over_hidden = (((1,), (1,)), ((), ()))

    @pl.when(step == 0)
    def _():
        out_ref[:, pl.ds(out_ref.shape[1] - lane_count, lane_count)] = gate_ref[...]

    gate_w = flat_rows(gate_w_ref)
    depth = gate_w.shape[0]
    out_ref[:, pl.ds(pl.multiple_of(step * depth, depth), depth)] = (
        lax.dot_general(
            units_ref[:, :hidden], gate_w, over_hidden, preferred_element_type=jnp.float32
        )
        + lax.dot_general(
            units_ref[:, hidden : 2 * hidden],
            flat_rows(up_w_ref),
            over_hidden,
            preferred_element_type=jnp.float32,
        )
    ).astype(jnp.bfloat16)


def input_parts(units, stacked, gate_part):
    rows = units.shape[0]
    hidden = stacked.shape[3]
    width = stacked.shape[0] * stacked.shape[2]
    depth = 512
    return pl.pallas_call(
        part_kernel,
        grid=(width // depth,),
        in_specs=[
            whole((rows, 3 * hidden)),
            weight_block(stacked, 0, depth, lambda i: i),
            weight_block(stacked, 1, depth, lambda i: i),
            whole((rows, lane_count)),
        ],
        out_specs=whole((rows, width + lane_count)),
        out_shape=jax.ShapeDtypeStruct((rows, width + lane_count), jnp.bfloat16),
        compiler_params=pltpu.CompilerParams(vmem_limit_bytes=vmem_bytes),
        cost_estimate=pl.CostEstimate(
            flops=4 * rows * width * hidden, bytes_accessed=10_000_000, transcendentals=0
        ),
    )(units, stacked, stacked, gate_part)


def adam_kernel(
    new_place_ref,
    old_place_ref,
    returned_ref,
    stored_ref,
    first_ref,
    second_ref,
    new_first_ref,
    new_second_ref,
    leaving_ref,
    row_ref,
    state_ref,
):
    slots, experts = returned_ref.shape[0], stored_ref.shape[1]
    first_scale = learn_rate / (1.0 - beta_one**adam_step)
    second_scale = 1.0 / (1.0 - beta_two**adam_step)
    for row in range(experts):
        row_ref[old_place_ref[row]] = row
    state_ref[...] = jnp.zeros_like(state_ref)
    for slot in range(slots):
        row = row_ref[new_place_ref[slot]]
        state_ref[row] = state_ref[row] + returned_ref[slot, 0].astype(jnp.float32)
    for row in range(experts):
        grad = state_ref[row]
        new_first = beta_one * first_ref[0, row] + (1.0 - beta_one) * grad
        new_second = beta_two * second_ref[0, row] + (1.0 - beta_two) * grad * grad
        new_first_ref[0, row] = new_first
        new_second_ref[0, row] = new_second
        state_ref[row] = stored_ref[0, row].astype(jnp.float32) - first_scale * new_first / (
            jnp.sqrt(second_scale * new_second) + adam_eps
        )
    for slot in range(slots):
        leaving_ref[slot, 0] = state_ref[row_ref[new_place_ref[slot]]].astype(jnp.bfloat16)


def adam_update(new_place, old_place, returned, stored, first, second):
    slots, matrices, rows, hidden = returned.shape
    experts = stored.shape[1]
    by_slot = pl.BlockSpec((slots, 1, rows, hidden), lambda i: (0, i, 0, 0))
    by_row = pl.BlockSpec((1, experts, rows, hidden), lambda i: (i, 0, 0, 0))
    scalars = pl.BlockSpec(memory_space=pltpu.SMEM)
    return pl.pallas_call(
        adam_kernel,
        grid=(matrices,),
        in_specs=[scalars, scalars, by_slot, by_row, by_row, by_row],
        out_specs=[by_row, by_row, by_slot],
        out_shape=[
            jax.ShapeDtypeStruct(first.shape, jnp.float32),
            jax.ShapeDtypeStruct(second.shape, jnp.float32),
            jax.ShapeDtypeStruct(returned.shape, jnp.bfloat16),
        ],
        scratch_shapes=[
            pltpu.SMEM((experts,), jnp.int32),
            pltpu.VMEM((experts, rows, hidden), jnp.float32),
        ],
        compiler_params=pltpu.CompilerParams(vmem_limit_bytes=vmem_bytes),
        cost_estimate=pl.CostEstimate(
            flops=20 * first.size, bytes_accessed=9_000_000, transcendentals=2 * first.size
        ),
    )(new_place, old_place, returned, stored, first, second)


def body(
    tokens, cotangent, routing, gates, new_place, old_place, weights, first_moment, second_moment
):
    tok_count, feature_width = tokens.shape
    top_count = routing.shape[1]
    expert_count = weights.shape[1]
    block_rows = weights.shape[2]
    hidden = weights.shape[3]
    slot_count = lax.axis_size("expert")
    capacity = 2 * tok_count * top_count // slot_count
    buffer_rows = slot_count * capacity
    source = lax.axis_index("expert")
    expert_ids = jnp.arange(expert_count, dtype=jnp.int32)
    slot_ids = jnp.arange(slot_count, dtype=jnp.int32)
    place_hot = (new_place[:, None] == expert_ids[None, :]).astype(jnp.int32)
    slot_state = (new_place[:, None] == old_place[None, :]).astype(jnp.bfloat16)

    outgoing = jnp.einsum(
        "se,cerh->scrh", slot_state, weights, preferred_element_type=jnp.float32
    ).astype(jnp.bfloat16)
    arrived = lax.all_to_all(outgoing, "expert", split_axis=0, concat_axis=0, tiled=True)

    replica_count = jnp.sum(place_hot, axis=0)
    earlier = jnp.cumsum(place_hot, axis=0) - place_hot
    slot_rank = jnp.sum(earlier * place_hot, axis=1)
    wanted = source % replica_count
    chosen = place_hot * (slot_rank[:, None] == wanted[None, :]).astype(jnp.int32)
    target_slot = jnp.sum(chosen * slot_ids[:, None], axis=0)
    flat_experts = routing.reshape(-1)
    assign_hot = (flat_experts[:, None] == expert_ids[None, :]).astype(jnp.int32)
    position = jnp.sum((jnp.cumsum(assign_hot, axis=0) - assign_hot) * assign_hot, axis=1)
    target = jnp.sum(assign_hot * target_slot[None, :], axis=1)
    destination = target * capacity + position
    assign_dest = (
        destination[:, None] == jnp.arange(buffer_rows, dtype=jnp.int32)[None, :]
    ).astype(jnp.bfloat16)
    token_dest = jnp.sum(assign_dest.reshape(tok_count, top_count, buffer_rows), axis=1)

    pair_rows = 2 * capacity
    first_row = (target * pair_rows + position).reshape(tok_count, top_count)
    row_of = jnp.concatenate([first_row, first_row + capacity])
    scale_of = jnp.concatenate([jnp.ones_like(gates), gates])
    message_rows = jnp.arange(slot_count * pair_rows, dtype=jnp.int32)
    both_dest = sum(
        jnp.where(row_of[:, k, None] == message_rows[None, :], scale_of[:, k, None], 0)
        for k in range(top_count)
    ).astype(jnp.bfloat16)
    packed = (
        jnp.einsum(
            "tb,td->bd",
            both_dest,
            jnp.concatenate([tokens, cotangent]),
            preferred_element_type=jnp.float32,
        )
        .astype(jnp.bfloat16)
        .reshape(slot_count, pair_rows, feature_width)
    )
    arrived, packed = lax.optimization_barrier((arrived, packed))
    stacked = lax.all_gather(
        jnp.transpose(arrived, (1, 0, 2, 3)).reshape(3, slot_count * block_rows, hidden),
        "dp",
        axis=0,
    )
    received = lax.all_to_all(packed, "expert", split_axis=0, concat_axis=0, tiled=True).reshape(
        slot_count, 2, capacity, feature_width
    )
    weight_grads, units, gate_part = unit_and_weight_grads(received, stacked)
    summed = lax.psum_scatter(weight_grads, "dp", scatter_dimension=1, tiled=True)
    pieces = jnp.transpose(summed.reshape(3, slot_count, block_rows, hidden), (1, 0, 2, 3))
    input_part = input_parts(units, stacked, gate_part)
    back = lax.all_to_all(
        input_part.reshape(slot_count, capacity, feature_width + lane_count),
        "expert",
        split_axis=0,
        concat_axis=0,
        tiled=True,
    ).reshape(buffer_rows, feature_width + lane_count)
    pieces, back = lax.optimization_barrier((pieces, back))
    input_grad = jnp.einsum(
        "tb,bd->td", token_dest, back[:, :feature_width], preferred_element_type=jnp.float32
    ).astype(jnp.bfloat16)
    gate_sum = jnp.einsum(
        "ab,bl->al", assign_dest, back[:, feature_width:], preferred_element_type=jnp.float32
    )[:, 0].reshape(tok_count, top_count)
    gate_grad = (gate_sum / gates.astype(jnp.float32)).astype(jnp.bfloat16)

    returned = lax.all_to_all(pieces, "expert", split_axis=0, concat_axis=0, tiled=True)
    new_first, new_second, leaving = adam_update(
        new_place, old_place, returned, weights, first_moment, second_moment
    )
    landed = lax.all_to_all(leaving, "expert", split_axis=0, concat_axis=0, tiled=True)
    slot_weights = jnp.transpose(landed, (1, 0, 2, 3)).reshape(
        3, 1, slot_count * block_rows, hidden
    )
    return (input_grad, gate_grad, slot_weights, new_first, new_second)


def solution(mesh):
    placed = (
        P(("dp", "expert"), None),
        P(("dp", "expert"), None),
        P(("dp", "expert"), None),
        P(("dp", "expert"), None),
        P(),
        P(),
        P(None, None, ("dp", "expert"), None),
        P(None, None, ("dp", "expert"), None),
        P(None, None, ("dp", "expert"), None),
    )
    return jax.shard_map(
        body,
        mesh=mesh,
        in_specs=placed,
        out_specs=(
            P(("dp", "expert"), None),
            P(("dp", "expert"), None),
            P(None, "expert", "dp", None),
            P(None, None, ("dp", "expert"), None),
            P(None, None, ("dp", "expert"), None),
        ),
        check_vma=False,
    )
```

```python
import jax
import jax.numpy as jnp
from jax import lax
from jax.experimental import pallas as pl
from jax.experimental.pallas import tpu as pltpu
from jax.sharding import PartitionSpec as P

beta_one = 0.9
beta_two = 0.95
learn_rate = 0.02
adam_step = 10.0
adam_eps = 1e-08


lane_count = 128
vmem_bytes = 60 * 1024 * 1024


def whole(shape):
    return pl.BlockSpec(shape, lambda i: (0,) * len(shape), pipeline_mode=pl.Buffered(1))


def flat_rows(ref):
    return ref[...].reshape(-1, ref.shape[-1])


def grad_kernel(
    steps,
    x_ref,
    y_ref,
    gate_w_ref,
    up_w_ref,
    down_w_ref,
    dw_ref,
    part_ref,
    first_ref,
    second_ref,
    u_ref,
    units_ref,
):
    step = pl.program_id(0)
    rows, hidden = u_ref.shape
    span_rows = 128
    width = part_ref.shape[1] - lane_count
    products = ((first_ref, x_ref, gate_w_ref), (second_ref, x_ref, up_w_ref), (u_ref, y_ref, down_w_ref))

    @pl.when(step == 0)
    def _():
        for total, left, right in products:
            total[...] = jnp.dot(
                flat_rows(left), flat_rows(right), preferred_element_type=jnp.float32
            )

    @pl.when((step > 0) & (step < steps))
    def _():
        for total, left, right in products:
            total[...] += jnp.dot(
                flat_rows(left), flat_rows(right), preferred_element_type=jnp.float32
            )

    @pl.when(step == steps - 1)
    def _():
        for start in range(0, rows, span_rows):
            span = pl.ds(start, span_rows)
            weighted = u_ref[span]
            first_pre = first_ref[span]
            second_pre = second_ref[span]
            sigmoid_h = jax.nn.sigmoid(first_pre)
            gated = first_pre * sigmoid_h
            activated = gated * second_pre
            total = jnp.sum(activated * weighted, axis=1, keepdims=True)
            grad_first = weighted * second_pre * sigmoid_h * (1.0 + first_pre * (1.0 - sigmoid_h))
            units_ref[span, :hidden] = grad_first.astype(jnp.bfloat16)
            units_ref[span, hidden : 2 * hidden] = (weighted * gated).astype(jnp.bfloat16)
            units_ref[span, 2 * hidden :] = activated.astype(jnp.bfloat16)
            part_ref[span, width:] = jnp.broadcast_to(total, (span_rows, lane_count)).astype(
                jnp.bfloat16
            )

    @pl.when(step >= steps)
    def _():
        both = jnp.dot(
            flat_rows(x_ref).T, units_ref[:, : 2 * hidden], preferred_element_type=jnp.float32
        ).astype(jnp.bfloat16)
        dw_ref[0] = both[:, :hidden]
        dw_ref[1] = both[:, hidden:]
        dw_ref[2] = jnp.dot(
            flat_rows(y_ref).T, units_ref[:, 2 * hidden :], preferred_element_type=jnp.float32
        ).astype(jnp.bfloat16)
        over_hidden = (((1,), (1,)), ((), ()))
        gate_w = flat_rows(gate_w_ref)
        depth = gate_w.shape[0]
        part_ref[:, pl.ds(pl.multiple_of((step - steps) * depth, depth), depth)] = (
            lax.dot_general(
                units_ref[:, :hidden], gate_w, over_hidden, preferred_element_type=jnp.float32
            )
            + lax.dot_general(
                units_ref[:, hidden : 2 * hidden],
                flat_rows(up_w_ref),
                over_hidden,
                preferred_element_type=jnp.float32,
            )
        ).astype(jnp.bfloat16)


def expert_rows(received, stacked):
    sources, _, capacity, width = received.shape
    _, _, stored_rows, hidden = stacked.shape
    rows = sources * capacity
    depth = 512
    steps = width // depth

    def row_block(which):
        return pl.BlockSpec(
            (sources, 1, capacity, depth), lambda i: (0, which, 0, lax.rem(i, steps))
        )

    def weight_block(matrix, block_of):
        return pl.BlockSpec(
            (depth // stored_rows, 1, stored_rows, hidden), lambda i: (block_of(i), matrix, 0, 0)
        )

    return pl.pallas_call(
        lambda *refs: grad_kernel(steps, *refs),
        grid=(2 * steps,),
        in_specs=[
            row_block(0),
            row_block(1),
            weight_block(0, lambda i: lax.rem(i, steps)),
            weight_block(1, lambda i: lax.rem(i, steps)),
            weight_block(2, lambda i: jnp.minimum(i, steps - 1)),
        ],
        out_specs=[
            pl.BlockSpec((3, depth, hidden), lambda i: (0, jnp.maximum(i - steps, 0), 0)),
            whole((rows, width + lane_count)),
        ],
        out_shape=[
            jax.ShapeDtypeStruct((3, width, hidden), jnp.bfloat16),
            jax.ShapeDtypeStruct((rows, width + lane_count), jnp.bfloat16),
        ],
        scratch_shapes=[pltpu.VMEM((rows, hidden), jnp.float32)] * 3
        + [pltpu.VMEM((rows, 3 * hidden), jnp.bfloat16)],
        compiler_params=pltpu.CompilerParams(vmem_limit_bytes=vmem_bytes),
        cost_estimate=pl.CostEstimate(
            flops=16 * rows * width * hidden,
            bytes_accessed=36_000_000,
            transcendentals=rows * hidden,
        ),
    )(received, received, stacked, stacked, stacked)


def adam_kernel(
    new_place_ref,
    old_place_ref,
    returned_ref,
    stored_ref,
    first_ref,
    second_ref,
    new_first_ref,
    new_second_ref,
    leaving_ref,
    row_ref,
    state_ref,
):
    slots, experts = returned_ref.shape[0], stored_ref.shape[1]
    first_scale = learn_rate / (1.0 - beta_one**adam_step)
    second_scale = 1.0 / (1.0 - beta_two**adam_step)
    for row in range(experts):
        row_ref[old_place_ref[row]] = row
    state_ref[...] = jnp.zeros_like(state_ref)
    for slot in range(slots):
        row = row_ref[new_place_ref[slot]]
        state_ref[row] = state_ref[row] + returned_ref[slot, 0].astype(jnp.float32)
    for row in range(experts):
        grad = state_ref[row]
        new_first = beta_one * first_ref[0, row] + (1.0 - beta_one) * grad
        new_second = beta_two * second_ref[0, row] + (1.0 - beta_two) * grad * grad
        new_first_ref[0, row] = new_first
        new_second_ref[0, row] = new_second
        state_ref[row] = stored_ref[0, row].astype(jnp.float32) - first_scale * new_first / (
            jnp.sqrt(second_scale * new_second) + adam_eps
        )
    for slot in range(slots):
        leaving_ref[slot, 0] = state_ref[row_ref[new_place_ref[slot]]].astype(jnp.bfloat16)


def adam_update(new_place, old_place, returned, stored, first, second):
    slots, matrices, rows, hidden = returned.shape
    experts = stored.shape[1]
    by_slot = pl.BlockSpec((slots, 1, rows, hidden), lambda i: (0, i, 0, 0))
    by_row = pl.BlockSpec((1, experts, rows, hidden), lambda i: (i, 0, 0, 0))
    scalars = pl.BlockSpec(memory_space=pltpu.SMEM)
    return pl.pallas_call(
        adam_kernel,
        grid=(matrices,),
        in_specs=[scalars, scalars, by_slot, by_row, by_row, by_row],
        out_specs=[by_row, by_row, by_slot],
        out_shape=[
            jax.ShapeDtypeStruct(first.shape, jnp.float32),
            jax.ShapeDtypeStruct(second.shape, jnp.float32),
            jax.ShapeDtypeStruct(returned.shape, jnp.bfloat16),
        ],
        scratch_shapes=[
            pltpu.SMEM((experts,), jnp.int32),
            pltpu.VMEM((experts, rows, hidden), jnp.float32),
        ],
        compiler_params=pltpu.CompilerParams(vmem_limit_bytes=vmem_bytes),
        cost_estimate=pl.CostEstimate(
            flops=20 * first.size, bytes_accessed=9_000_000, transcendentals=2 * first.size
        ),
    )(new_place, old_place, returned, stored, first, second)


def body(
    tokens, cotangent, routing, gates, new_place, old_place, weights, first_moment, second_moment
):
    tok_count, feature_width = tokens.shape
    top_count = routing.shape[1]
    expert_count = weights.shape[1]
    block_rows = weights.shape[2]
    hidden = weights.shape[3]
    slot_count = lax.axis_size("expert")
    capacity = 2 * tok_count * top_count // slot_count
    buffer_rows = slot_count * capacity
    source = lax.axis_index("expert")
    expert_ids = jnp.arange(expert_count, dtype=jnp.int32)
    slot_ids = jnp.arange(slot_count, dtype=jnp.int32)
    place_hot = (new_place[:, None] == expert_ids[None, :]).astype(jnp.int32)
    slot_state = (new_place[:, None] == old_place[None, :]).astype(jnp.bfloat16)

    outgoing = jnp.einsum(
        "se,cerh->scrh", slot_state, weights, preferred_element_type=jnp.float32
    ).astype(jnp.bfloat16)
    arrived = lax.all_to_all(outgoing, "expert", split_axis=0, concat_axis=0, tiled=True)

    replica_count = jnp.sum(place_hot, axis=0)
    earlier = jnp.cumsum(place_hot, axis=0) - place_hot
    slot_rank = jnp.sum(earlier * place_hot, axis=1)
    wanted = source % replica_count
    chosen = place_hot * (slot_rank[:, None] == wanted[None, :]).astype(jnp.int32)
    target_slot = jnp.sum(chosen * slot_ids[:, None], axis=0)
    flat_experts = routing.reshape(-1)
    assign_hot = (flat_experts[:, None] == expert_ids[None, :]).astype(jnp.int32)
    position = jnp.sum((jnp.cumsum(assign_hot, axis=0) - assign_hot) * assign_hot, axis=1)
    target = jnp.sum(assign_hot * target_slot[None, :], axis=1)
    destination = target * capacity + position
    assign_dest = (
        destination[:, None] == jnp.arange(buffer_rows, dtype=jnp.int32)[None, :]
    ).astype(jnp.bfloat16)
    token_dest = jnp.sum(assign_dest.reshape(tok_count, top_count, buffer_rows), axis=1)

    pair_rows = 2 * capacity
    first_row = (target * pair_rows + position).reshape(tok_count, top_count)
    row_of = jnp.concatenate([first_row, first_row + capacity])
    scale_of = jnp.concatenate([jnp.ones_like(gates), gates])
    message_rows = jnp.arange(slot_count * pair_rows, dtype=jnp.int32)
    both_dest = sum(
        jnp.where(row_of[:, k, None] == message_rows[None, :], scale_of[:, k, None], 0)
        for k in range(top_count)
    ).astype(jnp.bfloat16)
    packed = (
        jnp.einsum(
            "tb,td->bd",
            both_dest,
            jnp.concatenate([tokens, cotangent]),
            preferred_element_type=jnp.float32,
        )
        .astype(jnp.bfloat16)
        .reshape(slot_count, pair_rows, feature_width)
    )
    arrived, packed = lax.optimization_barrier((arrived, packed))
    stacked = lax.all_gather(
        jnp.transpose(arrived, (1, 0, 2, 3)).reshape(3, slot_count * block_rows, hidden),
        "dp",
        axis=0,
    )
    received = lax.all_to_all(packed, "expert", split_axis=0, concat_axis=0, tiled=True).reshape(
        slot_count, 2, capacity, feature_width
    )
    weight_grads, input_part = expert_rows(received, stacked)
    summed = lax.psum_scatter(weight_grads, "dp", scatter_dimension=1, tiled=True)
    pieces = jnp.transpose(summed.reshape(3, slot_count, block_rows, hidden), (1, 0, 2, 3))
    back = lax.all_to_all(
        input_part.reshape(slot_count, capacity, feature_width + lane_count),
        "expert",
        split_axis=0,
        concat_axis=0,
        tiled=True,
    ).reshape(buffer_rows, feature_width + lane_count)
    pieces, back = lax.optimization_barrier((pieces, back))
    input_grad = jnp.einsum(
        "tb,bd->td", token_dest, back[:, :feature_width], preferred_element_type=jnp.float32
    ).astype(jnp.bfloat16)
    gate_sum = jnp.einsum(
        "ab,bl->al", assign_dest, back[:, feature_width:], preferred_element_type=jnp.float32
    )[:, 0].reshape(tok_count, top_count)
    gate_grad = (gate_sum / gates.astype(jnp.float32)).astype(jnp.bfloat16)

    returned = lax.all_to_all(pieces, "expert", split_axis=0, concat_axis=0, tiled=True)
    new_first, new_second, leaving = adam_update(
        new_place, old_place, returned, weights, first_moment, second_moment
    )
    landed = lax.all_to_all(leaving, "expert", split_axis=0, concat_axis=0, tiled=True)
    slot_weights = jnp.transpose(landed, (1, 0, 2, 3)).reshape(
        3, 1, slot_count * block_rows, hidden
    )
    return (input_grad, gate_grad, slot_weights, new_first, new_second)


def solution(mesh):
    placed = (
        P(("dp", "expert"), None),
        P(("dp", "expert"), None),
        P(("dp", "expert"), None),
        P(("dp", "expert"), None),
        P(),
        P(),
        P(None, None, ("dp", "expert"), None),
        P(None, None, ("dp", "expert"), None),
        P(None, None, ("dp", "expert"), None),
    )
    return jax.shard_map(
        body,
        mesh=mesh,
        in_specs=placed,
        out_specs=(
            P(("dp", "expert"), None),
            P(("dp", "expert"), None),
            P(None, "expert", "dp", None),
            P(None, None, ("dp", "expert"), None),
            P(None, None, ("dp", "expert"), None),
        ),
        check_vma=False,
    )
```

```python
import jax
import jax.numpy as jnp
from jax import lax
from jax.experimental import pallas as pl
from jax.experimental.pallas import tpu as pltpu
from jax.sharding import PartitionSpec as P

beta_one = 0.9
beta_two = 0.95
learn_rate = 0.02
adam_step = 10.0
adam_eps = 1e-08


lane_count = 128
vmem_bytes = 60 * 1024 * 1024


def whole(shape):
    return pl.BlockSpec(shape, lambda i: (0,) * len(shape), pipeline_mode=pl.Buffered(1))


def flat_rows(ref):
    return ref[...].reshape(-1, ref.shape[-1])


def grad_kernel(
    steps,
    x_ref,
    y_ref,
    gate_w_ref,
    up_w_ref,
    down_w_ref,
    dw_ref,
    part_ref,
    first_ref,
    second_ref,
    u_ref,
    units_ref,
):
    step = pl.program_id(0)
    rows, hidden = u_ref.shape
    span_rows = 128
    width = part_ref.shape[1] - lane_count
    products = ((first_ref, x_ref, gate_w_ref), (second_ref, x_ref, up_w_ref), (u_ref, y_ref, down_w_ref))

    @pl.when(step == 0)
    def _():
        for total, left, right in products:
            total[...] = jnp.dot(
                flat_rows(left), flat_rows(right), preferred_element_type=jnp.float32
            )

    @pl.when((step > 0) & (step < steps))
    def _():
        for total, left, right in products:
            total[...] += jnp.dot(
                flat_rows(left), flat_rows(right), preferred_element_type=jnp.float32
            )

    @pl.when(step == steps - 1)
    def _():
        for start in range(0, rows, span_rows):
            span = pl.ds(start, span_rows)
            weighted = u_ref[span]
            first_pre = first_ref[span]
            second_pre = second_ref[span]
            sigmoid_h = jax.nn.sigmoid(first_pre)
            gated = first_pre * sigmoid_h
            activated = gated * second_pre
            total = jnp.sum(activated * weighted, axis=1, keepdims=True)
            grad_first = weighted * second_pre * sigmoid_h * (1.0 + first_pre * (1.0 - sigmoid_h))
            units_ref[span, :hidden] = grad_first.astype(jnp.bfloat16)
            units_ref[span, hidden : 2 * hidden] = (weighted * gated).astype(jnp.bfloat16)
            units_ref[span, 2 * hidden :] = activated.astype(jnp.bfloat16)
            part_ref[span, width:] = jnp.broadcast_to(total, (span_rows, lane_count)).astype(
                jnp.bfloat16
            )

    @pl.when(step >= steps)
    def _():
        both = jnp.dot(
            flat_rows(x_ref).T, units_ref[:, : 2 * hidden], preferred_element_type=jnp.float32
        ).astype(jnp.bfloat16)
        dw_ref[0] = both[:, :hidden]
        dw_ref[1] = both[:, hidden:]
        dw_ref[2] = jnp.dot(
            flat_rows(y_ref).T, units_ref[:, 2 * hidden :], preferred_element_type=jnp.float32
        ).astype(jnp.bfloat16)
        over_hidden = (((1,), (1,)), ((), ()))
        gate_w = flat_rows(gate_w_ref)
        depth = gate_w.shape[0]
        part_ref[:, pl.ds(pl.multiple_of((step - steps) * depth, depth), depth)] = (
            lax.dot_general(
                units_ref[:, :hidden], gate_w, over_hidden, preferred_element_type=jnp.float32
            )
            + lax.dot_general(
                units_ref[:, hidden : 2 * hidden],
                flat_rows(up_w_ref),
                over_hidden,
                preferred_element_type=jnp.float32,
            )
        ).astype(jnp.bfloat16)


def expert_rows(received, stacked):
    sources, _, capacity, width = received.shape
    _, _, stored_rows, hidden = stacked.shape
    rows = sources * capacity
    depth = 512
    steps = width // depth

    def row_block(which):
        return pl.BlockSpec(
            (sources, 1, capacity, depth), lambda i: (0, which, 0, lax.rem(i, steps))
        )

    def weight_block(matrix, block_of):
        return pl.BlockSpec(
            (depth // stored_rows, 1, stored_rows, hidden), lambda i: (block_of(i), matrix, 0, 0)
        )

    return pl.pallas_call(
        lambda *refs: grad_kernel(steps, *refs),
        grid=(2 * steps,),
        in_specs=[
            row_block(0),
            row_block(1),
            weight_block(0, lambda i: lax.rem(i, steps)),
            weight_block(1, lambda i: lax.rem(i, steps)),
            weight_block(2, lambda i: jnp.minimum(i, steps - 1)),
        ],
        out_specs=[
            pl.BlockSpec((3, depth, hidden), lambda i: (0, jnp.maximum(i - steps, 0), 0)),
            whole((rows, width + lane_count)),
        ],
        out_shape=[
            jax.ShapeDtypeStruct((3, width, hidden), jnp.bfloat16),
            jax.ShapeDtypeStruct((rows, width + lane_count), jnp.bfloat16),
        ],
        scratch_shapes=[pltpu.VMEM((rows, hidden), jnp.float32)] * 3
        + [pltpu.VMEM((rows, 3 * hidden), jnp.bfloat16)],
        compiler_params=pltpu.CompilerParams(vmem_limit_bytes=vmem_bytes),
        cost_estimate=pl.CostEstimate(
            flops=16 * rows * width * hidden,
            bytes_accessed=36_000_000,
            transcendentals=rows * hidden,
        ),
    )(received, received, stacked, stacked, stacked)


def adam_kernel(
    new_place_ref,
    old_place_ref,
    returned_ref,
    stored_ref,
    first_ref,
    second_ref,
    new_first_ref,
    new_second_ref,
    leaving_ref,
    row_ref,
    state_ref,
):
    slots, experts = returned_ref.shape[0], stored_ref.shape[1]
    first_scale = learn_rate / (1.0 - beta_one**adam_step)
    second_scale = 1.0 / (1.0 - beta_two**adam_step)
    for row in range(experts):
        row_ref[old_place_ref[row]] = row
    state_ref[...] = jnp.zeros_like(state_ref)
    for slot in range(slots):
        row = row_ref[new_place_ref[slot]]
        state_ref[row] = state_ref[row] + returned_ref[slot, 0].astype(jnp.float32)
    for row in range(experts):
        grad = state_ref[row]
        new_first = beta_one * first_ref[0, row] + (1.0 - beta_one) * grad
        new_second = beta_two * second_ref[0, row] + (1.0 - beta_two) * grad * grad
        new_first_ref[0, row] = new_first
        new_second_ref[0, row] = new_second
        state_ref[row] = stored_ref[0, row].astype(jnp.float32) - first_scale * new_first / (
            jnp.sqrt(second_scale * new_second) + adam_eps
        )
    for slot in range(slots):
        leaving_ref[slot, 0] = state_ref[row_ref[new_place_ref[slot]]].astype(jnp.bfloat16)


def adam_update(new_place, old_place, returned, stored, first, second):
    slots, matrices, rows, hidden = returned.shape
    experts = stored.shape[1]
    by_slot = pl.BlockSpec((slots, 1, rows, hidden), lambda i: (0, i, 0, 0))
    by_row = pl.BlockSpec((1, experts, rows, hidden), lambda i: (i, 0, 0, 0))
    scalars = pl.BlockSpec(memory_space=pltpu.SMEM)
    return pl.pallas_call(
        adam_kernel,
        grid=(matrices,),
        in_specs=[scalars, scalars, by_slot, by_row, by_row, by_row],
        out_specs=[by_row, by_row, by_slot],
        out_shape=[
            jax.ShapeDtypeStruct(first.shape, jnp.float32),
            jax.ShapeDtypeStruct(second.shape, jnp.float32),
            jax.ShapeDtypeStruct(returned.shape, jnp.bfloat16),
        ],
        scratch_shapes=[
            pltpu.SMEM((experts,), jnp.int32),
            pltpu.VMEM((experts, rows, hidden), jnp.float32),
        ],
        compiler_params=pltpu.CompilerParams(vmem_limit_bytes=vmem_bytes // 3),
        cost_estimate=pl.CostEstimate(
            flops=20 * first.size, bytes_accessed=9_000_000, transcendentals=2 * first.size
        ),
    )(new_place, old_place, returned, stored, first, second)


def slot_kernel(new_place_ref, old_place_ref, stored_ref, leaving_ref, row_ref):
    slots = leaving_ref.shape[0]
    for row in range(stored_ref.shape[1]):
        row_ref[old_place_ref[row]] = row
    for slot in range(slots):
        row = row_ref[new_place_ref[pl.program_id(0) * slots + slot]]
        leaving_ref[slot] = stored_ref[:, row]


def slot_rows(new_place, old_place, stored):
    slots = new_place.shape[0]
    matrices, experts, rows, hidden = stored.shape
    block = slots // 4
    scalars = pl.BlockSpec(memory_space=pltpu.SMEM)
    return pl.pallas_call(
        slot_kernel,
        grid=(slots // block,),
        in_specs=[scalars, scalars, whole(stored.shape)],
        out_specs=pl.BlockSpec((block, matrices, rows, hidden), lambda i: (i, 0, 0, 0)),
        out_shape=jax.ShapeDtypeStruct((slots, matrices, rows, hidden), jnp.bfloat16),
        scratch_shapes=[pltpu.SMEM((experts,), jnp.int32)],
        compiler_params=pltpu.CompilerParams(vmem_limit_bytes=vmem_bytes),
        cost_estimate=pl.CostEstimate(flops=0, bytes_accessed=2_000_000, transcendentals=0),
    )(new_place, old_place, stored)


def body(
    tokens, cotangent, routing, gates, new_place, old_place, weights, first_moment, second_moment
):
    tok_count, feature_width = tokens.shape
    top_count = routing.shape[1]
    expert_count = weights.shape[1]
    block_rows = weights.shape[2]
    hidden = weights.shape[3]
    slot_count = lax.axis_size("expert")
    capacity = 2 * tok_count * top_count // slot_count
    buffer_rows = slot_count * capacity
    source = lax.axis_index("expert")
    expert_ids = jnp.arange(expert_count, dtype=jnp.int32)
    slot_ids = jnp.arange(slot_count, dtype=jnp.int32)
    place_hot = (new_place[:, None] == expert_ids[None, :]).astype(jnp.int32)

    outgoing = slot_rows(new_place, old_place, weights)
    arrived = lax.all_to_all(outgoing, "expert", split_axis=0, concat_axis=0, tiled=True)

    replica_count = jnp.sum(place_hot, axis=0)
    earlier = jnp.cumsum(place_hot, axis=0) - place_hot
    slot_rank = jnp.sum(earlier * place_hot, axis=1)
    wanted = source % replica_count
    chosen = place_hot * (slot_rank[:, None] == wanted[None, :]).astype(jnp.int32)
    target_slot = jnp.sum(chosen * slot_ids[:, None], axis=0)
    flat_experts = routing.reshape(-1)
    assign_hot = (flat_experts[:, None] == expert_ids[None, :]).astype(jnp.int32)
    position = jnp.sum((jnp.cumsum(assign_hot, axis=0) - assign_hot) * assign_hot, axis=1)
    target = jnp.sum(assign_hot * target_slot[None, :], axis=1)
    destination = target * capacity + position
    assign_dest = (
        destination[:, None] == jnp.arange(buffer_rows, dtype=jnp.int32)[None, :]
    ).astype(jnp.bfloat16)
    token_dest = jnp.sum(assign_dest.reshape(tok_count, top_count, buffer_rows), axis=1)

    pair_rows = 2 * capacity
    first_row = (target * pair_rows + position).reshape(tok_count, top_count)
    row_of = jnp.concatenate([first_row, first_row + capacity])
    scale_of = jnp.concatenate([jnp.ones_like(gates), gates])
    message_rows = jnp.arange(slot_count * pair_rows, dtype=jnp.int32)
    both_dest = sum(
        jnp.where(row_of[:, k, None] == message_rows[None, :], scale_of[:, k, None], 0)
        for k in range(top_count)
    ).astype(jnp.bfloat16)
    packed = (
        jnp.einsum(
            "tb,td->bd",
            both_dest,
            jnp.concatenate([tokens, cotangent]),
            preferred_element_type=jnp.float32,
        )
        .astype(jnp.bfloat16)
        .reshape(slot_count, pair_rows, feature_width)
    )
    arrived, packed = lax.optimization_barrier((arrived, packed))
    stacked = lax.all_gather(
        jnp.transpose(arrived, (1, 0, 2, 3)).reshape(3, slot_count * block_rows, hidden),
        "dp",
        axis=0,
    )
    received = lax.all_to_all(packed, "expert", split_axis=0, concat_axis=0, tiled=True).reshape(
        slot_count, 2, capacity, feature_width
    )
    weight_grads, input_part = expert_rows(received, stacked)
    summed = lax.psum_scatter(weight_grads, "dp", scatter_dimension=1, tiled=True)
    pieces = jnp.transpose(summed.reshape(3, slot_count, block_rows, hidden), (1, 0, 2, 3))
    back = lax.all_to_all(
        input_part.reshape(slot_count, capacity, feature_width + lane_count),
        "expert",
        split_axis=0,
        concat_axis=0,
        tiled=True,
    ).reshape(buffer_rows, feature_width + lane_count)
    pieces, back = lax.optimization_barrier((pieces, back))
    input_grad = jnp.einsum(
        "tb,bd->td", token_dest, back[:, :feature_width], preferred_element_type=jnp.float32
    ).astype(jnp.bfloat16)
    gate_sum = jnp.einsum(
        "ab,bl->al", assign_dest, back[:, feature_width:], preferred_element_type=jnp.float32
    )[:, 0].reshape(tok_count, top_count)
    gate_grad = (gate_sum / gates.astype(jnp.float32)).astype(jnp.bfloat16)

    returned = lax.all_to_all(pieces, "expert", split_axis=0, concat_axis=0, tiled=True)
    new_first, new_second, leaving = adam_update(
        new_place, old_place, returned, weights, first_moment, second_moment
    )
    landed = lax.all_to_all(leaving, "expert", split_axis=0, concat_axis=0, tiled=True)
    slot_weights = jnp.transpose(landed, (1, 0, 2, 3)).reshape(
        3, 1, slot_count * block_rows, hidden
    )
    return (input_grad, gate_grad, slot_weights, new_first, new_second)


def solution(mesh):
    placed = (
        P(("dp", "expert"), None),
        P(("dp", "expert"), None),
        P(("dp", "expert"), None),
        P(("dp", "expert"), None),
        P(),
        P(),
        P(None, None, ("dp", "expert"), None),
        P(None, None, ("dp", "expert"), None),
        P(None, None, ("dp", "expert"), None),
    )
    return jax.shard_map(
        body,
        mesh=mesh,
        in_specs=placed,
        out_specs=(
            P(("dp", "expert"), None),
            P(("dp", "expert"), None),
            P(None, "expert", "dp", None),
            P(None, None, ("dp", "expert"), None),
            P(None, None, ("dp", "expert"), None),
        ),
        check_vma=False,
    )
```

```python
import jax
import jax.numpy as jnp
from jax import lax
from jax.experimental import pallas as pl
from jax.experimental.pallas import tpu as pltpu
from jax.sharding import PartitionSpec as P

beta_one = 0.9
beta_two = 0.95
learn_rate = 0.02
adam_step = 10.0
adam_eps = 1e-08


lane_count = 128
vmem_bytes = 60 * 1024 * 1024


def whole(shape):
    return pl.BlockSpec(shape, lambda i: (0,) * len(shape), pipeline_mode=pl.Buffered(1))


def flat_rows(ref):
    return ref[...].reshape(-1, ref.shape[-1])


def grad_kernel(
    steps,
    x_ref,
    y_ref,
    gate_w_ref,
    up_w_ref,
    down_w_ref,
    dw_ref,
    part_ref,
    first_ref,
    second_ref,
    u_ref,
    units_ref,
):
    step = pl.program_id(0)
    rows, hidden = u_ref.shape
    span_rows = 128
    width = part_ref.shape[1] - lane_count
    products = ((first_ref, x_ref, gate_w_ref), (second_ref, x_ref, up_w_ref), (u_ref, y_ref, down_w_ref))

    @pl.when(step == 0)
    def _():
        for total, left, right in products:
            total[...] = jnp.dot(
                flat_rows(left), flat_rows(right), preferred_element_type=jnp.float32
            )

    @pl.when((step > 0) & (step < steps))
    def _():
        for total, left, right in products:
            total[...] += jnp.dot(
                flat_rows(left), flat_rows(right), preferred_element_type=jnp.float32
            )

    @pl.when(step == steps - 1)
    def _():
        for start in range(0, rows, span_rows):
            span = pl.ds(start, span_rows)
            weighted = u_ref[span]
            first_pre = first_ref[span]
            second_pre = second_ref[span]
            sigmoid_h = jax.nn.sigmoid(first_pre)
            gated = first_pre * sigmoid_h
            activated = gated * second_pre
            total = jnp.sum(activated * weighted, axis=1, keepdims=True)
            grad_first = weighted * second_pre * sigmoid_h * (1.0 + first_pre * (1.0 - sigmoid_h))
            units_ref[span, :hidden] = grad_first.astype(jnp.bfloat16)
            units_ref[span, hidden : 2 * hidden] = (weighted * gated).astype(jnp.bfloat16)
            units_ref[span, 2 * hidden :] = activated.astype(jnp.bfloat16)
            part_ref[span, width:] = jnp.broadcast_to(total, (span_rows, lane_count)).astype(
                jnp.bfloat16
            )

    @pl.when(step >= steps)
    def _():
        both = jnp.dot(
            flat_rows(x_ref).T, units_ref[:, : 2 * hidden], preferred_element_type=jnp.float32
        ).astype(jnp.bfloat16)
        dw_ref[0] = both[:, :hidden]
        dw_ref[1] = both[:, hidden:]
        dw_ref[2] = jnp.dot(
            flat_rows(y_ref).T, units_ref[:, 2 * hidden :], preferred_element_type=jnp.float32
        ).astype(jnp.bfloat16)
        over_hidden = (((1,), (1,)), ((), ()))
        gate_w = flat_rows(gate_w_ref)
        depth = gate_w.shape[0]
        part_ref[:, pl.ds(pl.multiple_of((step - steps) * depth, depth), depth)] = (
            lax.dot_general(
                units_ref[:, :hidden], gate_w, over_hidden, preferred_element_type=jnp.float32
            )
            + lax.dot_general(
                units_ref[:, hidden : 2 * hidden],
                flat_rows(up_w_ref),
                over_hidden,
                preferred_element_type=jnp.float32,
            )
        ).astype(jnp.bfloat16)


def expert_rows(received, stacked):
    sources, _, capacity, width = received.shape
    _, _, stored_rows, hidden = stacked.shape
    rows = sources * capacity
    depth = 512
    steps = width // depth

    def row_block(which):
        return pl.BlockSpec(
            (sources, 1, capacity, depth), lambda i: (0, which, 0, lax.rem(i, steps))
        )

    def weight_block(matrix, block_of):
        return pl.BlockSpec(
            (depth // stored_rows, 1, stored_rows, hidden), lambda i: (block_of(i), matrix, 0, 0)
        )

    return pl.pallas_call(
        lambda *refs: grad_kernel(steps, *refs),
        grid=(2 * steps,),
        in_specs=[
            row_block(0),
            row_block(1),
            weight_block(0, lambda i: lax.rem(i, steps)),
            weight_block(1, lambda i: lax.rem(i, steps)),
            weight_block(2, lambda i: jnp.minimum(i, steps - 1)),
        ],
        out_specs=[
            pl.BlockSpec((3, depth, hidden), lambda i: (0, jnp.maximum(i - steps, 0), 0)),
            whole((rows, width + lane_count)),
        ],
        out_shape=[
            jax.ShapeDtypeStruct((3, width, hidden), jnp.bfloat16),
            jax.ShapeDtypeStruct((rows, width + lane_count), jnp.bfloat16),
        ],
        scratch_shapes=[pltpu.VMEM((rows, hidden), jnp.float32)] * 3
        + [pltpu.VMEM((rows, 3 * hidden), jnp.bfloat16)],
        compiler_params=pltpu.CompilerParams(vmem_limit_bytes=vmem_bytes * 3 // 4),
        cost_estimate=pl.CostEstimate(
            flops=16 * rows * width * hidden,
            bytes_accessed=36_000_000,
            transcendentals=rows * hidden,
        ),
    )(received, received, stacked, stacked, stacked)


def adam_kernel(
    new_place_ref,
    old_place_ref,
    returned_ref,
    stored_ref,
    first_ref,
    second_ref,
    new_first_ref,
    new_second_ref,
    leaving_ref,
    row_ref,
    state_ref,
):
    slots, experts = returned_ref.shape[0], stored_ref.shape[1]
    first_scale = learn_rate / (1.0 - beta_one**adam_step)
    second_scale = 1.0 / (1.0 - beta_two**adam_step)
    for row in range(experts):
        row_ref[old_place_ref[row]] = row
    state_ref[...] = jnp.zeros_like(state_ref)
    for slot in range(slots):
        row = row_ref[new_place_ref[slot]]
        state_ref[row] = state_ref[row] + returned_ref[slot, 0].astype(jnp.float32)
    for row in range(experts):
        grad = state_ref[row]
        new_first = beta_one * first_ref[0, row] + (1.0 - beta_one) * grad
        new_second = beta_two * second_ref[0, row] + (1.0 - beta_two) * grad * grad
        new_first_ref[0, row] = new_first
        new_second_ref[0, row] = new_second
        state_ref[row] = stored_ref[0, row].astype(jnp.float32) - first_scale * new_first / (
            jnp.sqrt(second_scale * new_second) + adam_eps
        )
    for slot in range(slots):
        leaving_ref[slot, 0] = state_ref[row_ref[new_place_ref[slot]]].astype(jnp.bfloat16)


def adam_update(new_place, old_place, returned, stored, first, second):
    slots, matrices, rows, hidden = returned.shape
    experts = stored.shape[1]
    by_slot = pl.BlockSpec((slots, 1, rows, hidden), lambda i: (0, i, 0, 0))
    by_row = pl.BlockSpec((1, experts, rows, hidden), lambda i: (i, 0, 0, 0))
    scalars = pl.BlockSpec(memory_space=pltpu.SMEM)
    return pl.pallas_call(
        adam_kernel,
        grid=(matrices,),
        in_specs=[scalars, scalars, by_slot, by_row, by_row, by_row],
        out_specs=[by_row, by_row, by_slot],
        out_shape=[
            jax.ShapeDtypeStruct(first.shape, jnp.float32),
            jax.ShapeDtypeStruct(second.shape, jnp.float32),
            jax.ShapeDtypeStruct(returned.shape, jnp.bfloat16),
        ],
        scratch_shapes=[
            pltpu.SMEM((experts,), jnp.int32),
            pltpu.VMEM((experts, rows, hidden), jnp.float32),
        ],
        compiler_params=pltpu.CompilerParams(vmem_limit_bytes=vmem_bytes // 3),
        cost_estimate=pl.CostEstimate(
            flops=20 * first.size, bytes_accessed=9_000_000, transcendentals=2 * first.size
        ),
    )(new_place, old_place, returned, stored, first, second)


def slot_kernel(new_place_ref, old_place_ref, stored_ref, leaving_ref, row_ref):
    slots = leaving_ref.shape[0]
    for row in range(stored_ref.shape[1]):
        row_ref[old_place_ref[row]] = row
    for slot in range(slots):
        row = row_ref[new_place_ref[pl.program_id(0) * slots + slot]]
        leaving_ref[slot] = stored_ref[:, row]


def slot_rows(new_place, old_place, stored):
    slots = new_place.shape[0]
    matrices, experts, rows, hidden = stored.shape
    block = slots // 4
    scalars = pl.BlockSpec(memory_space=pltpu.SMEM)
    return pl.pallas_call(
        slot_kernel,
        grid=(slots // block,),
        in_specs=[scalars, scalars, whole(stored.shape)],
        out_specs=pl.BlockSpec((block, matrices, rows, hidden), lambda i: (i, 0, 0, 0)),
        out_shape=jax.ShapeDtypeStruct((slots, matrices, rows, hidden), jnp.bfloat16),
        scratch_shapes=[pltpu.SMEM((experts,), jnp.int32)],
        compiler_params=pltpu.CompilerParams(vmem_limit_bytes=vmem_bytes),
        cost_estimate=pl.CostEstimate(flops=0, bytes_accessed=2_000_000, transcendentals=0),
    )(new_place, old_place, stored)


def body(
    tokens, cotangent, routing, gates, new_place, old_place, weights, first_moment, second_moment
):
    tok_count, feature_width = tokens.shape
    top_count = routing.shape[1]
    expert_count = weights.shape[1]
    block_rows = weights.shape[2]
    hidden = weights.shape[3]
    slot_count = lax.axis_size("expert")
    capacity = 2 * tok_count * top_count // slot_count
    buffer_rows = slot_count * capacity
    source = lax.axis_index("expert")
    expert_ids = jnp.arange(expert_count, dtype=jnp.int32)
    slot_ids = jnp.arange(slot_count, dtype=jnp.int32)
    place_hot = (new_place[:, None] == expert_ids[None, :]).astype(jnp.int32)

    outgoing = slot_rows(new_place, old_place, weights)
    arrived = lax.all_to_all(outgoing, "expert", split_axis=0, concat_axis=0, tiled=True)

    replica_count = jnp.sum(place_hot, axis=0)
    earlier = jnp.cumsum(place_hot, axis=0) - place_hot
    slot_rank = jnp.sum(earlier * place_hot, axis=1)
    wanted = source % replica_count
    chosen = place_hot * (slot_rank[:, None] == wanted[None, :]).astype(jnp.int32)
    target_slot = jnp.sum(chosen * slot_ids[:, None], axis=0)
    flat_experts = routing.reshape(-1)
    assign_hot = (flat_experts[:, None] == expert_ids[None, :]).astype(jnp.int32)
    position = jnp.sum((jnp.cumsum(assign_hot, axis=0) - assign_hot) * assign_hot, axis=1)
    target = jnp.sum(assign_hot * target_slot[None, :], axis=1)
    destination = target * capacity + position
    assign_dest = (
        destination[:, None] == jnp.arange(buffer_rows, dtype=jnp.int32)[None, :]
    ).astype(jnp.bfloat16)
    token_dest = jnp.sum(assign_dest.reshape(tok_count, top_count, buffer_rows), axis=1)

    pair_rows = 2 * capacity
    first_row = (target * pair_rows + position).reshape(tok_count, top_count)
    row_of = jnp.concatenate([first_row, first_row + capacity])
    scale_of = jnp.concatenate([jnp.ones_like(gates), gates])
    message_rows = jnp.arange(slot_count * pair_rows, dtype=jnp.int32)
    both_dest = sum(
        jnp.where(row_of[:, k, None] == message_rows[None, :], scale_of[:, k, None], 0)
        for k in range(top_count)
    ).astype(jnp.bfloat16)
    packed = (
        jnp.einsum(
            "tb,td->bd",
            both_dest,
            jnp.concatenate([tokens, cotangent]),
            preferred_element_type=jnp.float32,
        )
        .astype(jnp.bfloat16)
        .reshape(slot_count, pair_rows, feature_width)
    )
    arrived, packed = lax.optimization_barrier((arrived, packed))
    stacked = lax.all_gather(
        jnp.transpose(arrived, (1, 0, 2, 3)).reshape(3, slot_count * block_rows, hidden),
        "dp",
        axis=0,
    )
    received = lax.all_to_all(packed, "expert", split_axis=0, concat_axis=0, tiled=True).reshape(
        slot_count, 2, capacity, feature_width
    )
    weight_grads, input_part = expert_rows(received, stacked)
    summed = lax.psum_scatter(weight_grads, "dp", scatter_dimension=1, tiled=True)
    pieces = jnp.transpose(summed.reshape(3, slot_count, block_rows, hidden), (1, 0, 2, 3))
    back = lax.all_to_all(
        input_part.reshape(slot_count, capacity, feature_width + lane_count),
        "expert",
        split_axis=0,
        concat_axis=0,
        tiled=True,
    ).reshape(buffer_rows, feature_width + lane_count)
    pieces, back = lax.optimization_barrier((pieces, back))
    input_grad = jnp.einsum(
        "tb,bd->td", token_dest, back[:, :feature_width], preferred_element_type=jnp.float32
    ).astype(jnp.bfloat16)
    gate_sum = jnp.einsum(
        "ab,bl->al", assign_dest, back[:, feature_width:], preferred_element_type=jnp.float32
    )[:, 0].reshape(tok_count, top_count)
    gate_grad = (gate_sum / gates.astype(jnp.float32)).astype(jnp.bfloat16)

    returned = lax.all_to_all(pieces, "expert", split_axis=0, concat_axis=0, tiled=True)
    new_first, new_second, leaving = adam_update(
        new_place, old_place, returned, weights, first_moment, second_moment
    )
    landed = lax.all_to_all(leaving, "expert", split_axis=0, concat_axis=0, tiled=True)
    slot_weights = jnp.transpose(landed, (1, 0, 2, 3)).reshape(
        3, 1, slot_count * block_rows, hidden
    )
    return (input_grad, gate_grad, slot_weights, new_first, new_second)


def solution(mesh):
    placed = (
        P(("dp", "expert"), None),
        P(("dp", "expert"), None),
        P(("dp", "expert"), None),
        P(("dp", "expert"), None),
        P(),
        P(),
        P(None, None, ("dp", "expert"), None),
        P(None, None, ("dp", "expert"), None),
        P(None, None, ("dp", "expert"), None),
    )
    return jax.shard_map(
        body,
        mesh=mesh,
        in_specs=placed,
        out_specs=(
            P(("dp", "expert"), None),
            P(("dp", "expert"), None),
            P(None, "expert", "dp", None),
            P(None, None, ("dp", "expert"), None),
            P(None, None, ("dp", "expert"), None),
        ),
        check_vma=False,
    )
```
